512 devices in a mesh: dp: 128 (over z_lo, x, y, core), tensor: 4 (over z_hi).
Axes of the slice: x: 4, y: 8, z: 8 (z_hi: 4, z_lo: 2; z = z_hi * 2 + z_lo), core: 2. Of those that a mesh axis runs over, the one named last changes fastest.
Arguments:
- hidden_states: bfloat16 [16384, 5376], P('dp', 'tensor'), may hold values from -2 to 2
- embedding: bfloat16 [4096, 5376], P(('dp', 'tensor')), may hold values from -6 to 6
- targets: int32 [16384], P('dp'), may hold values from 0 to 4095
- prior_lse: float32 [16384], P('dp'), may hold values from 9 to 15
Outputs:
- loss: float32 [16384], P('dp')
- hidden_grad: bfloat16 [16384, 5376], P('dp', 'tensor')
The draws below stay inside these ranges and needn't reach their ends.
All inputs are finite; a program needn't handle non-finite values.
Results may differ from the reference program's by a relative error of at most 0.012.
Values may be sent and summed in bfloat16 or wider, within the bound.
A program may use at most 64 MiB of HBM per device.

```python
import math
import jax
import jax.numpy as jnp
from jax import lax

D = 5376
TOK_DEV = 128
VROW = 8
TOKENS = 16384
VBLOCK = 4096
N_DP = 128
N_TENSOR = 4


def base_table(key):
    return jnp.clip(jax.random.normal(key, (VBLOCK, D), jnp.float32), -6.0, 6.0)


def draw_embedding(key, part):
    table = base_table(key)
    return table.astype(jnp.bfloat16)


def draw_hidden_states(key, part):
    key = jax.random.fold_in(key, 7)
    keys = jax.random.split(key, 1)
    bound_value = 2.0
    values = jax.random.normal(keys[0], (TOKENS, D), jnp.float32) * (3.0 / math.sqrt(D))
    return jnp.clip(values, -bound_value, bound_value).astype(jnp.bfloat16)


def set_ends(values, own_key, least, largest):
    longest = values.shape.index(max(values.shape))
    spots = []
    for shift in (0, 1):
        where = [jax.random.randint(jax.random.fold_in(own_key, axis), (), 0, length) for axis, length in enumerate(values.shape)]
        where[longest] = (where[longest] + shift) % values.shape[longest]
        spots.append(tuple(where))
    return values.at[spots[0]].set(least).at[spots[1]].set(largest)


def block_levels(own_key, dims, cuts, smallest, top_value):
    factor_of = 1.0
    for axis_at, parts in cuts:
        steps = jax.random.uniform(jax.random.fold_in(jax.random.fold_in(own_key, 6), axis_at), (parts,), jnp.float32, smallest / len(cuts), top_value / len(cuts))
        factor_of = factor_of * jnp.repeat(jnp.exp(steps), dims[axis_at] // parts).reshape((-1,) + (1,) * (len(dims) - 1 - axis_at))
    return factor_of


def setup_inputs(seed: int = 0) -> dict:
    key_list = jax.random.split(jax.random.key(seed), 5)
    return {
        "hidden_states": draw_hidden_states(jax.random.fold_in(key_list[4], 71), 0),
        "embedding": draw_embedding(jax.random.fold_in(key_list[4], 71), 0),
        "targets": set_ends(jax.random.randint(key_list[2], (TOKENS,), 0, VBLOCK), jax.random.fold_in(key_list[2], 1), 0, VBLOCK - 1).astype(jnp.int32),
        "prior_lse": jnp.clip(9.0 + 6.0 * jax.random.uniform(key_list[3], (TOKENS,), jnp.float32) ** block_levels(key_list[3], (TOKENS,), ((0, 128),), -0.2, 0.2), 9.0, 15.0),
    }


def token_block(embedding, block):
    hidden, target, prior = block
    logits = jnp.dot(hidden, embedding.T, preferred_element_type=jnp.float32)
    row_peak = jnp.maximum(jnp.max(logits, axis=1), prior)
    total = jnp.sum(jnp.exp(logits - row_peak[:, None]), axis=1) + jnp.exp(prior - row_peak)
    lse = row_peak + jnp.log(total)
    columns = jnp.arange(logits.shape[1], dtype=jnp.int32)
    one_hot = (columns[None, :] == target[:, None]).astype(jnp.float32)
    target_logit = jnp.sum(logits * one_hot, axis=1)
    loss = lse - target_logit
    grad_logits = (jnp.exp(logits - lse[:, None]) - one_hot).astype(jnp.bfloat16)
    count = hidden.shape[0]
    grad_four = grad_logits.reshape(count, N_DP, N_TENSOR, VROW)
    table_four = embedding.reshape(N_DP, N_TENSOR, VROW, D)
    summed = jnp.zeros((count, D), jnp.float32)
    for quarter in range(N_TENSOR):
        grad_part = grad_four[:, :, quarter].reshape(count, N_DP * VROW)
        table_part = table_four[:, quarter].reshape(N_DP * VROW, D)
        partial_value = jnp.dot(grad_part, table_part, preferred_element_type=jnp.float32).astype(jnp.bfloat16)
        partial_value = lax.optimization_barrier(partial_value)
        summed = summed + partial_value.astype(jnp.float32)
    return loss, summed.astype(jnp.bfloat16)


def reference(hidden_states, embedding, targets, prior_lse):
    blocks = (hidden_states.reshape(N_DP, TOK_DEV, D), targets.reshape(N_DP, TOK_DEV), prior_lse.reshape(N_DP, TOK_DEV))
    loss, hidden_grad = lax.map(lambda block: token_block(embedding, block), blocks)
    return loss.reshape(TOKENS), hidden_grad.reshape(TOKENS, D)
```

```python
import jax
import jax.numpy as jnp
from jax import lax
from jax.experimental import pallas as pl
from jax.experimental.pallas import tpu as pltpu
from jax.sharding import PartitionSpec as P

MESH = pl.DeviceIdType.MESH
BF16 = jnp.bfloat16
F32 = jnp.float32
NX, NY, NZ, NK = 4, 8, 8, 4
D = 5376
QUARTER = D // NK
HALF = D // 2
TOK = 128
SET = TOK // NK
PIECE = 16
BLOCK = 8 * PIECE
ROWS = NY * NZ * PIECE


def device(x, y, z, c):
    return (((z % 2) * NX + x) * NY + y) * 2 + c, z // 2


def at_row(row):
    return pl.ds(pl.multiple_of(row * PIECE, PIECE), PIECE)


def ring_offset(m):
    return ((m + 1) // 2) * (1 - 2 * (m % 2))


def kernel(
    hid, emb, tgt, pri, loss, out,
    g, ebuf, hb, ht, lt, gl, meta, stat, lbuf, part, r1, s2, r2, zs, zr,
    e_s, g_r, s_r, p1_s, p2_s, s_s, ha_s, ha_r, hx_s, hx_r, hr_s, hr_r,
    m_s, m_r, t_s, t_r, l_s, l_r, o_s, o_r, d_s, d_r, q_s, q_r, z_s, z_r,
):
    dp = lax.axis_index("dp")
    k = lax.axis_index("tensor")
    c = dp % 2
    y = dp // 2 % NY
    x = dp // (2 * NY) % NX
    zl = dp // (2 * NY * NX)
    z = 2 * k + zl
    first = c == 0

    def x_dev(d):
        return device((x + d) % NX, y, z, c)

    def k_dev(kk):
        return device(x, y, 2 * kk + zl, c)

    sibling = device(x, y, z, 1 - c)

    outer, inner = jnp.where(first, z, y), jnp.where(first, y, z)

    def ring_dev(o, i):
        return device(x, jnp.where(first, i, o), jnp.where(first, o, i), c)

    inner_next = ring_dev(outer, (inner + 1) % 8)
    inner_last = ring_dev(outer, (inner + 7) % 8)
    outer_next = ring_dev((outer + 1) % 8, inner)
    outer_last = ring_dev((outer + 7) % 8, inner)

    partners = [sibling, inner_next, inner_last, outer_next, outer_last]
    partners += [x_dev(d) for d in (1, 2, 3)] + [k_dev((k + d) % NK) for d in (1, 2, 3)]
    barrier = pltpu.get_barrier_semaphore()
    for partner in partners:
        pl.semaphore_signal(barrier, inc=1, device_id=partner, device_id_type=MESH)
    pl.semaphore_wait(barrier, len(partners))

    def copy(src, dst, send, recv, where):
        return pltpu.make_async_remote_copy(
            src_ref=src, dst_ref=dst, send_sem=send, recv_sem=recv,
            device_id=where, device_id_type=MESH,
        )

    e_copy = copy(emb, ebuf, e_s.at[0], e_s.at[1], sibling)
    e_copy.start()

    def set_rows(kk):
        return pl.ds(pl.multiple_of(kk * SET, SET), SET)

    def hidden_set(d):
        kk = (k + d) % NK
        return copy(hid.at[set_rows(kk)], hb.at[x, k], ha_s.at[d - 1], ha_r.at[d - 1], k_dev(kk))

    for d in (2, 1, 3):
        hidden_set(d).start()
    hb[x, k] = hid[set_rows(k), :]

    def hidden_x(j, way):
        ref = hb.at[x, j]
        return copy(ref, ref, hx_s.at[way, j], hx_r.at[way, j], x_dev(1 - 2 * way + NX))

    for way in (0, 1):
        hidden_x(k, way).start()

    t = tgt[...]
    b = t // 8
    t_dp, t_k = b // 4, b % 4
    t_z = 2 * t_k + t_dp // (2 * NY * NX)
    place = (t_dp // (2 * NY) % NX) * ROWS + (t_z * NY + t_dp // 2 % NY) * PIECE + t_dp % 2 * 8 + t % 8
    meta[x] = jnp.concatenate([place.astype(F32), pri[...], jnp.zeros((6, TOK), F32)], axis=0)

    def to_x(buf, send, recv, d):
        return copy(buf.at[x], buf.at[x], send.at[d - 1], recv.at[d - 1], x_dev(d))

    for d in (1, 2, 3):
        to_x(meta, m_s, m_r, d).start()

    e_copy.wait()
    mine, other = emb[...], ebuf[...]
    rows = jnp.concatenate(
        [jnp.where(first, mine, other), jnp.where(first, other, mine)], axis=0
    )
    g[0, at_row(z * NY + y), :] = rows[:, :HALF]
    g[1, at_row(y * NZ + z), :] = rows[:, HALF:]

    def piece(o, i):
        return g.at[c, at_row(o * 8 + i)]

    def from_ring(o, i):
        ref = piece(o, i)
        copy(ref, ref, e_s.at[0], g_r.at[o * 8 + i], outer_next).wait_recv()

    def to_ring(o, i, send, where):
        ref = piece(o, i)
        return copy(ref, ref, send, g_r.at[o * 8 + i], where)

    def to_sibling(o, i):
        ref = piece(o, i)
        return copy(ref, ref, s_s.at[o * 8 + i], s_r.at[o * 8 + i], sibling)

    def from_sibling(o, i):
        ref = g.at[1 - c, at_row(o * 8 + i)]
        copy(ref, ref, s_s.at[0], s_r.at[o * 8 + i], sibling).wait_recv()

    def to_outer(m):
        i = (inner + ring_offset(m) + 8) % 8
        to_ring(outer, i, p2_s.at[0, m], outer_next).start()
        to_ring(outer, i, p2_s.at[1, m], outer_last).start()

    to_ring(outer, inner, p1_s.at[0, 0], inner_next).start()
    to_ring(outer, inner, p1_s.at[1, 0], inner_last).start()
    to_outer(0)
    for s in range(1, 5):
        i = (inner + 8 - s) % 8
        from_ring(outer, i)
        if s < 4:
            to_ring(outer, i, p1_s.at[0, s], inner_next).start()
        to_outer(2 * s - 1)
        to_sibling(outer, i).start()
        if s < 4:
            i = (inner + s) % 8
            from_ring(outer, i)
            if s < 3:
                to_ring(outer, i, p1_s.at[1, s], inner_last).start()
            to_outer(2 * s)
            to_sibling(outer, i).start()

    def second(ring, last):
        up, down = (outer + 8 - ring) % 8, (outer + ring) % 8

        def step(m, carry):
            i = (inner + ring_offset(m) + 8) % 8

            def pass_on(o, way, where):
                to_ring(o, i, p2_s.at[way, ring * 8 + m], where).start()

            from_ring(up, i)
            if last:
                pl.when(m < 4)(lambda: pass_on(up, 0, outer_next))
            else:
                pass_on(up, 0, outer_next)
            to_sibling(up, i).start()
            from_ring(down, i)
            if last:
                pl.when(m >= 4)(lambda: pass_on(down, 1, outer_last))
            else:
                pass_on(down, 1, outer_last)
            to_sibling(down, i).start()
            return carry

        lax.fori_loop(0, 8, step, 0)

    for d in (2, 1, 3):
        hidden_set(d).wait()
        for way in (0, 1):
            hidden_x((k + NK - d) % NK, way).start()

    second(1, False)

    def hidden_pass(j):
        way = j // 2
        ref = hb.at[(x + NX - 1 + 2 * way) % NX, j]
        return copy(ref, ref, hr_s.at[j], hr_r.at[j], x_dev(1 - 2 * way + NX))

    for j in range(NK):
        for way in (0, 1):
            hidden_x(j, way).wait()
        hidden_pass(j).start()

    second(2, False)

    for j in range(NK):
        hidden_pass(j).wait()
    for xx in range(NX):
        for h in (0, 1):
            ht[h, xx * SET:(xx + 1) * SET, :] = jnp.concatenate(
                [hb[xx, 2 * h], hb[xx, 2 * h + 1]], axis=1
            )

    def logits(h, o):
        where = pl.ds(pl.multiple_of(o * BLOCK, BLOCK), BLOCK)
        lt[h, where, :] = lax.dot_general(
            g[h, where, :], ht[h], (((1,), (1,)), ((), ())), preferred_element_type=F32
        )

    def sibling_block(r):
        o = (inner + r) % 8

        def wait(m, carry):
            i = (outer + m) % 8
            pl.when((r != 0) | (m != 0))(lambda: from_sibling(o, i))
            return carry

        lax.fori_loop(0, 8, wait, 0)
        logits(1 - c, o)

    def early(n, carry):
        r = (n + 6) % 8
        logits(c, (outer + r) % 8)
        sibling_block(r)
        return carry

    lax.fori_loop(0, 5, early, 0)

    second(3, True)

    across = (outer + 4) % 8

    def final(m, carry):
        i = (inner + ring_offset(m) + 8) % 8
        from_ring(across, i)
        to_sibling(across, i).start()
        return carry

    for m in (0, 4, 1, 5, 2, 6, 3, 7):
        final(m, 0)

    def late(n, carry):
        r = n + 3
        logits(c, (outer + r) % 8)
        sibling_block(r)
        return carry

    lax.fori_loop(0, 3, late, 0)

    lane_set = lax.broadcasted_iota(jnp.int32, (8, TOK), 1) // SET
    for d in (1, 2, 3):
        to_x(meta, m_s, m_r, d).wait()
    info = jnp.zeros((8, TOK), F32)
    for xx in range(NX):
        turned = pltpu.roll(meta[xx], (xx + NX - k) % NX * SET, axis=1)
        info = jnp.where(lane_set == xx, turned, info)
    column = info[0:1] - (x * ROWS).astype(F32)
    prior = info[1:2]

    peak = jnp.full((1, TOK), -jnp.inf, F32)
    for zz in range(NZ):
        for yy in range(NY):
            r0, r1_ = (zz * NY + yy) * PIECE, (yy * NZ + zz) * PIECE
            value = lt[0, r0:r0 + PIECE, :] + lt[1, r1_:r1_ + PIECE, :]
            lt[0, r0:r0 + PIECE, :] = value
            peak = jnp.maximum(peak, jnp.max(value, axis=0, keepdims=True))
    total = jnp.zeros((8, TOK), F32)
    target = jnp.zeros((8, TOK), F32)
    row_id = lax.broadcasted_iota(jnp.int32, (BLOCK, TOK), 0).astype(F32)
    for n in range(8):
        value = lt[0, n * BLOCK:(n + 1) * BLOCK, :]
        hit = row_id == column - float(n * BLOCK)
        power = jnp.exp(value - peak)
        lt[0, n * BLOCK:(n + 1) * BLOCK, :] = power
        total += jnp.sum(power.reshape(BLOCK // 8, 8, TOK), axis=0)
        target += jnp.sum(jnp.where(hit, value, 0.0).reshape(BLOCK // 8, 8, TOK), axis=0)
    stat[x] = jnp.concatenate(
        [peak, jnp.sum(total, axis=0, keepdims=True), jnp.sum(target, axis=0, keepdims=True),
         jnp.zeros((5, TOK), F32)], axis=0,
    )
    for d in (1, 2, 3):
        to_x(stat, t_s, t_r, d).start()
    for d in (1, 2, 3):
        to_x(stat, t_s, t_r, d).wait()
    top = prior
    for xx in range(NX):
        top = jnp.maximum(top, stat[xx, 0:1, :])
    whole = jnp.exp(prior - top)
    logit = jnp.zeros((1, TOK), F32)
    for xx in range(NX):
        whole += stat[xx, 1:2, :] * jnp.exp(stat[xx, 0:1, :] - top)
        logit += stat[xx, 2:3, :]
    lse = top + jnp.log(whole)
    lbuf[k] = jnp.broadcast_to(lse - logit, (8, TOK))

    def loss_to(d):
        return copy(lbuf.at[k], lbuf.at[k], l_s.at[d - 1], l_r.at[d - 1], k_dev((k + d) % NK))

    for d in (1, 2, 3):
        loss_to(d).start()

    scale = jnp.exp(peak - lse)
    for n in range(8):
        hit = row_id == column - float(n * BLOCK)
        value = lt[0, n * BLOCK:(n + 1) * BLOCK, :] * scale - jnp.where(hit, 1.0, 0.0)
        gl[0, :, n * BLOCK:(n + 1) * BLOCK] = value.T.astype(BF16)
        for yy in range(NY):
            r = (yy * NZ + n) * PIECE
            lt[1, r:r + PIECE, :] = value[yy * PIECE:(yy + 1) * PIECE]
    for n in range(8):
        gl[1, :, n * BLOCK:(n + 1) * BLOCK] = lt[1, n * BLOCK:(n + 1) * BLOCK, :].T.astype(BF16)

    def x_rows(d):
        return pl.ds(pl.multiple_of((x + d) % NX * SET, SET), SET)

    half_order = [1 - k // 2, k // 2]

    def quarter(n):
        return 2 * half_order[n // 2] + n % 2

    def ahead(n):
        return 1 if n % 2 == 0 else 3

    def opposite_copy(n):
        j = quarter(n)
        return copy(part.at[j, x_rows(2)], r1.at[j], o_s.at[n], o_r.at[n], x_dev(ahead(n)))

    def direct_copy(n):
        j, d = quarter(n), 4 - ahead(n)
        return copy(part.at[j, x_rows(d)], r2.at[0, j], d_s.at[n], d_r.at[n], x_dev(d))

    def sum_copy(n):
        j = quarter(n)
        return copy(s2.at[j], r2.at[1, j], q_s.at[n], q_r.at[n], x_dev(ahead(n)))

    def z_copy(n):
        j = quarter(n)
        return copy(zs.at[j], zr.at[k], z_s.at[n], z_r.at[k], k_dev(j))

    def multiply(n):
        h, j = half_order[n // 2], quarter(n)
        lo = 0 if n % 2 == 0 else HALF - 1408
        value = jnp.dot(gl[h], g[h, :, lo:lo + 1408], preferred_element_type=F32).astype(BF16)
        part[j] = value[:, :QUARTER] if n % 2 == 0 else value[:, 1408 - QUARTER:]
        opposite_copy(n).start()
        direct_copy(n).start()

    def add_first(n):
        j = quarter(n)
        opposite_copy(n).wait()
        s2[j] = (part[j, x_rows(ahead(n)), :].astype(F32) + r1[j].astype(F32)).astype(BF16)
        sum_copy(n).start()

    def add_last(n):
        j = quarter(n)
        direct_copy(n).wait()
        sum_copy(n).wait()
        value = part[j, x_rows(0), :].astype(F32) + r2[0, j].astype(F32) + r2[1, j].astype(F32)
        zs[j] = value.astype(BF16)

        @pl.when(j == k)
        def _():
            zr[k] = value.astype(BF16)

        @pl.when(j != k)
        def _():
            z_copy(n).start()

    multiply(0)
    multiply(1)
    add_first(0)
    multiply(2)
    add_first(1)
    multiply(3)
    add_first(2)
    add_last(0)
    add_first(3)
    add_last(1)
    add_last(2)
    add_last(3)

    for d in (1, 2, 3):
        loss_to(d).wait()
    result = jnp.zeros((8, TOK), F32)
    for kk in range(NK):
        turned = pltpu.roll(lbuf[kk], (kk + NX - x) % NX * SET, axis=1)
        result = jnp.where(lane_set == kk, turned, result)
    loss[...] = result[0:1]

    for n in range(NK):
        @pl.when(quarter(n) != k)
        def _():
            z_copy(n).wait_send()
    for d in (1, 2, 3):
        kk = (k + d) % NK
        copy(zr.at[kk], zr.at[kk], z_s.at[0], z_r.at[kk], k_dev(kk)).wait_recv()
    for kk in range(NK):
        out[kk * SET:(kk + 1) * SET, :] = zr[kk]

    def sent(send):
        ref = piece(outer, inner)
        copy(ref, ref, send, g_r.at[0], outer_next).wait_send()

    for s in range(4):
        sent(p1_s.at[0, s])
        if s < 3:
            sent(p1_s.at[1, s])

    def sent_second(n, carry):
        sent(p2_s.at[0, n])
        sent(p2_s.at[1, n])
        return carry

    lax.fori_loop(0, 24, sent_second, 0)
    for m in range(4):
        sent(p2_s.at[0, 24 + m])
        sent(p2_s.at[1, 28 + m])

    def sent_sibling(n, carry):
        pl.when(n != outer * 8 + inner)(lambda: sent(s_s.at[n]))
        return carry

    lax.fori_loop(0, 64, sent_sibling, 0)


def body(hidden_states, embedding, targets, prior_lse):
    dma = pltpu.SemaphoreType.DMA
    vmem = pl.BlockSpec(memory_space=pltpu.VMEM)
    loss, grad = pl.pallas_call(
        kernel,
        out_shape=(
            jax.ShapeDtypeStruct((1, TOK), F32),
            jax.ShapeDtypeStruct((TOK, QUARTER), BF16),
        ),
        in_specs=[vmem] * 4,
        out_specs=(vmem, vmem),
        scratch_shapes=[
            pltpu.VMEM((2, ROWS, HALF), BF16),
            pltpu.VMEM((8, D), BF16),
            pltpu.VMEM((NX, NK, SET, QUARTER), BF16),
            pltpu.VMEM((2, TOK, HALF), BF16),
            pltpu.VMEM((2, ROWS, TOK), F32),
            pltpu.VMEM((2, TOK, ROWS), BF16),
            pltpu.VMEM((NX, 8, TOK), F32),
            pltpu.VMEM((NX, 8, TOK), F32),
            pltpu.VMEM((NK, 8, TOK), F32),
            pltpu.VMEM((NK, TOK, QUARTER), BF16),
            pltpu.VMEM((NK, SET, QUARTER), BF16),
            pltpu.VMEM((NK, SET, QUARTER), BF16),
            pltpu.VMEM((2, NK, SET, QUARTER), BF16),
            pltpu.VMEM((NK, SET, QUARTER), BF16),
            pltpu.VMEM((NK, SET, QUARTER), BF16),
            dma((2,)), dma((64,)), dma((64,)), dma((2, 4)), dma((2, 32)), dma((64,)),
            dma((3,)), dma((3,)), dma((2, 4)), dma((2, 4)), dma((4,)), dma((4,)),
            dma((3,)), dma((3,)), dma((3,)), dma((3,)), dma((3,)), dma((3,)),
            dma((4,)), dma((4,)), dma((4,)), dma((4,)), dma((4,)), dma((4,)), dma((4,)), dma((4,)),
        ],
        compiler_params=pltpu.CompilerParams(
            collective_id=0, has_side_effects=True, vmem_limit_bytes=48 << 20
        ),
        cost_estimate=pl.CostEstimate(
            flops=4 * TOK * ROWS * D, bytes_accessed=4 * TOK * D, transcendentals=TOK * ROWS
        ),
    )(hidden_states, embedding, targets.reshape(1, TOK), prior_lse.reshape(1, TOK))
    return loss.reshape(TOK), grad


def solution(mesh):
    placed = (P("dp", "tensor"), P(("dp", "tensor"), None), P("dp"), P("dp"))
    return jax.shard_map(
        body, mesh=mesh, in_specs=placed, out_specs=(P("dp"), P("dp", "tensor")), check_vma=False
    )
```

```python
import functools

import jax
import jax.numpy as jnp
from jax import lax
from jax.experimental import pallas as pl
from jax.experimental.pallas import tpu as pltpu
from jax.sharding import PartitionSpec as P

MESH = pl.DeviceIdType.MESH
BF16 = jnp.bfloat16
F32 = jnp.float32
NX, NY, NZ, NK = 4, 8, 8, 4
D = 5376
QUARTER = D // NK
MAIN = QUARTER // 128 * 128
REST = QUARTER - MAIN
SPLIT = 19 * 128
TOK = 128
SET = TOK // NK
SUB = SET // 2
PIECE = 16
BLOCK = 8 * PIECE
ROWS = NY * NZ * PIECE


def device(x, y, z, c):
    return (((z % 2) * NX + x) * NY + y) * 2 + c, z // 2


def at_row(row):
    return pl.ds(pl.multiple_of(row * PIECE, PIECE), PIECE)


def ring_offset(m):
    return ((m + 1) // 2) * (1 - 2 * (m % 2))


def rearranged(quarters):
    return jnp.concatenate(
        [q[:, :MAIN] for q in quarters] + [q[:, MAIN:] for q in quarters], axis=1
    )


def kernel(
    hid, emb, tgt, pri, loss, out,
    g, ebuf, hidn, hb, ht, lt, gl, raw, coef, meta, stat, lbuf, part, r1, s2, rd, rs, r3, zs, zr,
    e_s, g_r, s_r, g_s, s_s, ha_s, ha_r, hx_s, hx_r,
    m_s, m_r, t_s, t_r, l_s, l_r, o_s, o_r, d_s, d_r, q_s, q_r, w_s, w_r, z_s, z_r,
):
    dp = lax.axis_index("dp")
    k = lax.axis_index("tensor")
    c = dp % 2
    y = dp // 2 % NY
    x = dp // (2 * NY) % NX
    zl = dp // (2 * NY * NX)
    z = 2 * k + zl

    def x_dev(d):
        return device((x + d) % NX, y, z, c)

    def k_dev(kk):
        return device(x, y, 2 * kk + zl, c)

    sibling = device(x, y, z, 1 - c)

    partners = [sibling]
    partners += [device(x, (y + d) % NY, z, c) for d in (1, 7)]
    partners += [device(x, y, (z + d) % NZ, c) for d in (1, 7)]
    partners += [x_dev(d) for d in (1, 2, 3)] + [k_dev((k + d) % NK) for d in (1, 2, 3)]
    barrier = pltpu.get_barrier_semaphore()
    for partner in partners:
        pl.semaphore_signal(barrier, inc=1, device_id=partner, device_id_type=MESH)

    for lo in range(0, QUARTER, 128):
        hi = min(lo + 128, QUARTER)
        hidn[:, lo:hi] = hid[lo:hi, :].astype(F32).T.astype(BF16)
    t = tgt[...]
    b = t // 8
    t_dp, t_k = b // 4, b % 4
    t_z = 2 * t_k + t_dp // (2 * NY * NX)
    place = (t_dp // (2 * NY) % NX) * ROWS + (t_z * NY + t_dp // 2 % NY) * PIECE + t_dp % 2 * 8 + t % 8
    meta[x] = jnp.concatenate([place.astype(F32), pri[...], jnp.zeros((6, TOK), F32)], axis=0)
    pl.semaphore_wait(barrier, len(partners))

    def copy(src, dst, send, recv, where):
        return pltpu.make_async_remote_copy(
            src_ref=src, dst_ref=dst, send_sem=send, recv_sem=recv,
            device_id=where, device_id_type=MESH,
        )

    e_copy = copy(emb, ebuf, e_s.at[0], e_s.at[1], sibling)
    e_copy.start()

    def set_rows(kk):
        return pl.ds(pl.multiple_of(kk * SET, SET), SET)

    def hidden_set(d):
        kk = (k + d) % NK
        return copy(hidn.at[set_rows(kk)], hb.at[x, k], ha_s.at[d - 1], ha_r.at[d - 1], k_dev(kk))

    def hidden_x(j, d):
        ref = hb.at[x, j]
        return copy(ref, ref, hx_s.at[d - 1, j], hx_r.at[d - 1, j], x_dev(d))

    def hidden_on(d):
        hidden_set(d).wait()
        for e in (1, 3, 2):
            hidden_x((k + NK - d) % NK, e).start()

    def to_x(buf, send, recv, d):
        return copy(buf.at[x], buf.at[x], send.at[d - 1], recv.at[d - 1], x_dev(d))

    hb[x, k] = hidn[set_rows(k), :]
    e_copy.wait()
    mine, other = emb[...], ebuf[...]
    rows = jnp.concatenate(
        [jnp.where(c == 0, mine, other), jnp.where(c == 0, other, mine)], axis=0
    )
    g[at_row(z * NY + y), :] = rearranged(
        [rows[:, j * QUARTER:(j + 1) * QUARTER] for j in range(NK)]
    )

    def bring_in(h):
        outer, inner = (z, y) if h == 0 else (y, z)
        spans = (slice(0, SPLIT), slice(SPLIT, D))

        def number(o, i):
            return o * 8 + i if h == 0 else i * 8 + o

        def ring_dev(o, i):
            return device(x, i, o, c) if h == 0 else device(x, o, i, c)

        inner_next = ring_dev(outer, (inner + 1) % 8)
        inner_last = ring_dev(outer, (inner + 7) % 8)
        outer_next = ring_dev((outer + 1) % 8, inner)
        outer_last = ring_dev((outer + 7) % 8, inner)

        def piece(n, share):
            return g.at[at_row(n), spans[share]]

        def from_ring(o, i):
            ref = piece(number(o, i), h)
            copy(ref, ref, g_s.at[0], g_r.at[number(o, i)], outer_next).wait_recv()

        def to_ring(o, i, where):
            ref = piece(number(o, i), h)
            copy(ref, ref, g_s.at[0], g_r.at[number(o, i)], where).start()

        def to_sibling(o, i):
            ref = piece(number(o, i), h)
            copy(ref, ref, s_s.at[0], s_r.at[number(o, i)], sibling).start()

        def to_outer(m):
            i = (inner + ring_offset(m) + 8) % 8
            to_ring(outer, i, outer_next)
            to_ring(outer, i, outer_last)

        to_ring(outer, inner, inner_next)
        to_ring(outer, inner, inner_last)
        to_outer(0)
        for e in (1, 3, 2):
            hidden_x(k, e).start()
        for d in (1, 3, 2):
            hidden_set(d).start()
        for d in (1, 2, 3):
            to_x(meta, m_s, m_r, d).start()
        for s in range(1, 5):
            i = (inner + 8 - s) % 8
            from_ring(outer, i)
            if s < 4:
                to_ring(outer, i, inner_next)
            to_outer(2 * s - 1)
            to_sibling(outer, i)
            if s < 4:
                i = (inner + s) % 8
                from_ring(outer, i)
                if s < 3:
                    to_ring(outer, i, inner_last)
                to_outer(2 * s)
                to_sibling(outer, i)
            if s == 2:
                hidden_on(1)
                hidden_on(3)
            if s == 3:
                hidden_on(2)

        def second(ring, first, end):
            up, down = (outer + 8 - ring) % 8, (outer + ring) % 8

            def step(m, carry):
                i = (inner + ring_offset(m) + 8) % 8
                from_ring(up, i)
                if ring == 3:
                    pl.when(m < 4)(lambda: to_ring(up, i, outer_next))
                else:
                    to_ring(up, i, outer_next)
                to_sibling(up, i)
                from_ring(down, i)
                if ring == 3:
                    pl.when(m >= 4)(lambda: to_ring(down, i, outer_last))
                else:
                    to_ring(down, i, outer_last)
                to_sibling(down, i)
                return carry

            lax.fori_loop(first, end, step, 0)

        def logits(share, offsets):
            o0 = outer if share == h else inner
            by_z = share == 0
            starts = []
            for r in offsets:
                o = (o0 + r) % 8
                if by_z:
                    starts.append((pl.multiple_of(o * BLOCK, BLOCK), BLOCK))
                else:
                    starts += [(pl.multiple_of((i * 8 + o) * PIECE, PIECE), PIECE) for i in range(8)]
            left = jnp.concatenate([g[pl.ds(a, n), spans[share]] for a, n in starts], axis=0)
            value = lax.dot_general(
                left, ht[:, spans[share]], (((1,), (1,)), ((), ())), preferred_element_type=F32
            )
            at = 0
            for a, n in starts:
                lt[share, pl.ds(a, n), :] = value[at:at + n]
                at += n

        def await_sibling(r, skip):
            o = (inner + r) % 8

            def wait(m, carry):
                n = number((outer + m) % 8, o)
                ref = piece(n, 1 - h)
                copy(ref, ref, s_s.at[0], s_r.at[n], sibling).wait_recv()
                return carry

            lax.fori_loop(skip, 8, wait, 0)

        second(1, 0, 8)
        second(2, 0, 8)
        for j in range(NK):
            for d in (1, 2, 3):
                hidden_x(j, d).wait()
        for xx in range(NX):
            ht[xx * SET:(xx + 1) * SET, :] = rearranged([hb[xx, j] for j in range(NK)])

        def early(r, carry):
            second(3, 4 * (r - 1), 4 * r)
            logits(h, (r, 8 - r))
            await_sibling(r, 0)
            await_sibling(8 - r, 0)
            logits(1 - h, (r, 8 - r))
            return carry

        lax.fori_loop(1, 3, early, 0)
        logits(h, (3, 5))
        logits(h, (0,))
        await_sibling(0, 1)
        logits(1 - h, (0,))
        await_sibling(3, 0)
        await_sibling(5, 0)
        logits(1 - h, (3, 5))
        across = (outer + 4) % 8
        for m in (0, 4, 1, 5, 2, 6, 3, 7):
            i = (inner + ring_offset(m) + 8) % 8
            from_ring(across, i)
            to_sibling(across, i)
        logits(h, (4,))
        await_sibling(4, 0)
        logits(1 - h, (4,))

        ref = g.at[0:ROWS - PIECE, spans[h]]
        copy(ref, ref, g_s.at[0], g_r.at[0], outer_next).wait_send()
        copy(ref, ref, s_s.at[0], s_r.at[0], sibling).wait_send()

    for core in (0, 1):
        pl.when(c == core)(functools.partial(bring_in, core))

    lane_set = lax.broadcasted_iota(jnp.int32, (8, TOK), 1) // SET
    for d in (1, 2, 3):
        to_x(meta, m_s, m_r, d).wait()
    info = jnp.zeros((8, TOK), F32)
    for xx in range(NX):
        turned = pltpu.roll(meta[xx], (xx + NX - k) % NX * SET, axis=1)
        info = jnp.where(lane_set == xx, turned, info)
    column = info[0:1] - (x * ROWS).astype(F32)
    owned = (column >= 0.0) & (column < float(ROWS))
    prior = info[1:2]

    peaks = jnp.full((8, TOK), -jnp.inf, F32)
    for n in range(8):
        span = slice(n * BLOCK, (n + 1) * BLOCK)
        value = lt[0, span, :] + lt[1, span, :]
        lt[0, span, :] = value
        peaks = jnp.maximum(peaks, jnp.max(value.reshape(BLOCK // 8, 8, TOK), axis=0))
    peak = jnp.max(peaks, axis=0, keepdims=True)
    total = jnp.zeros((8, TOK), F32)
    target = jnp.zeros((8, TOK), F32)
    row_id = lax.broadcasted_iota(jnp.int32, (BLOCK, TOK), 0).astype(F32)
    for n in range(8):
        span = slice(n * BLOCK, (n + 1) * BLOCK)
        value = lt[0, span, :]
        hit = row_id == column - float(n * BLOCK)
        power = jnp.exp(value - peak)
        lt[1, span, :] = jnp.where(hit, 0.0, power)
        total += jnp.sum(power.reshape(BLOCK // 8, 8, TOK), axis=0)
        target += jnp.sum(jnp.where(hit, value, 0.0).reshape(BLOCK // 8, 8, TOK), axis=0)
    my_target = jnp.sum(target, axis=0, keepdims=True)
    stat[x] = jnp.concatenate(
        [peak, jnp.sum(total, axis=0, keepdims=True), my_target, jnp.zeros((5, TOK), F32)], axis=0
    )
    for d in (1, 2, 3):
        to_x(stat, t_s, t_r, d).start()

    column_t = jnp.broadcast_to(column, (8, TOK)).T[:, 0:1]
    lane_id = lax.broadcasted_iota(jnp.int32, (TOK, BLOCK), 1).astype(F32)
    for n in range(8):
        span = slice(n * BLOCK, (n + 1) * BLOCK)
        gl[0:TOK, span] = lt[1, span, :].T.astype(BF16)
        gl[TOK:, span] = jnp.where(lane_id == column_t - float(n * BLOCK), 1.0, 0.0).astype(BF16)

    quarters = [(k + 2) % NK, (k + 1) % NK, (k + 3) % NK, k]

    def products(n, use):
        j = quarters[n]
        for lo in range(0, MAIN, 256):
            at = pl.ds(pl.multiple_of(j * MAIN + lo, 128), 256)
            use(lo, jnp.dot(gl[...], g[:, at], preferred_element_type=F32))
        at = pl.ds(pl.multiple_of(NK * MAIN + j // 2 * 128, 128), 128)
        value = jnp.dot(gl[...], g[:, at], preferred_element_type=F32)
        use(MAIN, pltpu.roll(value, j % 2 * REST, axis=1)[:, :REST])

    def weigh(n):
        def use(lo, value):
            width = value.shape[1]
            for at in range(0, width, 128):
                w = min(128, width - at)
                mixed = (
                    value[:TOK, at:at + w] * coef[0, :, :w] + value[TOK:, at:at + w] * coef[1, :, :w]
                )
                part[n, :, lo + at:lo + at + w] = mixed.astype(BF16)
        return use

    def keep(lo, value):
        raw[:, lo:lo + value.shape[1]] = value

    products(0, keep)

    for d in (1, 2, 3):
        to_x(stat, t_s, t_r, d).wait()
    top = prior
    for xx in range(NX):
        top = jnp.maximum(top, stat[xx, 0:1, :])
    whole = jnp.exp(prior - top)
    logit = jnp.zeros((1, TOK), F32)
    for xx in range(NX):
        whole += stat[xx, 1:2, :] * jnp.exp(stat[xx, 0:1, :] - top)
        logit += stat[xx, 2:3, :]
    lse = top + jnp.log(whole)
    weights = jnp.concatenate(
        [jnp.exp(peak - lse), jnp.where(owned, jnp.exp(my_target - lse) - 1.0, 0.0),
         jnp.zeros((6, TOK), F32)], axis=0,
    ).T
    coef[0] = jnp.broadcast_to(weights[:, 0:1], (TOK, 128))
    coef[1] = jnp.broadcast_to(weights[:, 1:2], (TOK, 128))

    def x_rows(d):
        return pl.ds(pl.multiple_of((x + d) % NX * SET, SET), SET)

    def x_half(d, way):
        return pl.ds(pl.multiple_of((x + d) % NX * SET + way * SUB, SUB), SUB)

    ways = ((0, 1, 3), (1, 3, 1))
    last = NK - 1

    def opposite_copy(n, way, d):
        return copy(part.at[n, x_half(2, way)], r1.at[n, way], o_s.at[n, way], o_r.at[n, way], x_dev(d))

    def direct_copy(n, way, d):
        return copy(part.at[n, x_half(d, way)], rd.at[n, way], d_s.at[n, way], d_r.at[n, way], x_dev(d))

    def sum_copy(n, way, d):
        return copy(s2.at[n, way], rs.at[n, way], q_s.at[n, way], q_r.at[n, way], x_dev(d))

    def straight_copy(d):
        return copy(part.at[last, x_rows(d)], r3.at[d - 1], w_s.at[d - 1], w_r.at[d - 1], x_dev(d))

    def z_copy(n):
        return copy(zs.at[n], zr.at[n], z_s.at[n], z_r.at[n], k_dev(quarters[n]))

    def send_first(n):
        if n == last:
            for d in (2, 1, 3):
                straight_copy(d).start()
            return
        for way, near, _ in ways:
            opposite_copy(n, way, near).start()
        for way, _, far in ways:
            direct_copy(n, way, far).start()

    def add_first(n):
        for way, near, _ in ways:
            opposite_copy(n, way, near).wait()
            s2[n, way] = (part[n, x_half(near, way), :].astype(F32) + r1[n, way].astype(F32)).astype(BF16)
            sum_copy(n, way, near).start()

    def add_last(n):
        for way, near, far in ways:
            direct_copy(n, way, far).wait()
            sum_copy(n, way, near).wait()
            zs[n, way * SUB:(way + 1) * SUB, :] = (
                part[n, x_half(0, way), :].astype(F32) + rd[n, way].astype(F32) + rs[n, way].astype(F32)
            ).astype(BF16)
        z_copy(n).start()

    for lo in range(0, QUARTER, 128):
        w = min(128, QUARTER - lo)
        part[0, :, lo:lo + w] = (
            raw[:TOK, lo:lo + w] * coef[0, :, :w] + raw[TOK:, lo:lo + w] * coef[1, :, :w]
        ).astype(BF16)
    send_first(0)
    lbuf[k] = jnp.broadcast_to(lse - logit, (8, TOK))

    def loss_to(d):
        return copy(lbuf.at[k], lbuf.at[k], l_s.at[d - 1], l_r.at[d - 1], k_dev((k + d) % NK))

    for d in (1, 2, 3):
        loss_to(d).start()
    products(1, weigh(1))
    send_first(1)
    add_first(0)
    products(2, weigh(2))
    send_first(2)
    add_first(1)
    products(3, weigh(3))
    send_first(3)
    add_first(2)
    add_last(0)
    add_last(1)

    for d in (1, 2, 3):
        loss_to(d).wait()
    result = jnp.zeros((8, TOK), F32)
    for kk in range(NK):
        turned = pltpu.roll(lbuf[kk], (kk + NX - x) % NX * SET, axis=1)
        result = jnp.where(lane_set == kk, turned, result)
    loss[...] = result[0:1]

    add_last(2)
    for n in range(2):
        z_copy(n).wait()
        out[set_rows((k + (2, 3)[n]) % NK), :] = zr[n]
    for d in (1, 2, 3):
        straight_copy(d).wait()
    value = part[last, x_rows(0), :].astype(F32)
    for d in (1, 2, 3):
        value += r3[d - 1].astype(F32)
    out[set_rows(k), :] = value.astype(BF16)
    z_copy(2).wait()
    out[set_rows((k + 1) % NK), :] = zr[2]


def body(hidden_states, embedding, targets, prior_lse):
    dma = pltpu.SemaphoreType.DMA
    vmem = pl.BlockSpec(memory_space=pltpu.VMEM)
    loss, grad = pl.pallas_call(
        kernel,
        out_shape=(
            jax.ShapeDtypeStruct((1, TOK), F32),
            jax.ShapeDtypeStruct((TOK, QUARTER), BF16),
        ),
        in_specs=[vmem] * 4,
        out_specs=(vmem, vmem),
        scratch_shapes=[
            pltpu.VMEM((ROWS, D), BF16),
            pltpu.VMEM((8, D), BF16),
            pltpu.VMEM((TOK, QUARTER), BF16),
            pltpu.VMEM((NX, NK, SET, QUARTER), BF16),
            pltpu.VMEM((TOK, D), BF16),
            pltpu.VMEM((2, ROWS, TOK), F32),
            pltpu.VMEM((2 * TOK, ROWS), BF16),
            pltpu.VMEM((2 * TOK, QUARTER), F32),
            pltpu.VMEM((2, TOK, 128), F32),
            pltpu.VMEM((NX, 8, TOK), F32),
            pltpu.VMEM((NX, 8, TOK), F32),
            pltpu.VMEM((NK, 8, TOK), F32),
            pltpu.VMEM((NK, TOK, QUARTER), BF16),
            pltpu.VMEM((NK - 1, 2, SUB, QUARTER), BF16),
            pltpu.VMEM((NK - 1, 2, SUB, QUARTER), BF16),
            pltpu.VMEM((NK - 1, 2, SUB, QUARTER), BF16),
            pltpu.VMEM((NK - 1, 2, SUB, QUARTER), BF16),
            pltpu.VMEM((NX - 1, SET, QUARTER), BF16),
            pltpu.VMEM((NK - 1, SET, QUARTER), BF16),
            pltpu.VMEM((NK - 1, SET, QUARTER), BF16),
            dma((2,)), dma((64,)), dma((64,)), dma((1,)), dma((1,)),
            dma((3,)), dma((3,)), dma((3, 4)), dma((3, 4)),
            dma((3,)), dma((3,)), dma((3,)), dma((3,)), dma((3,)), dma((3,)),
            dma((3, 2)), dma((3, 2)), dma((3, 2)), dma((3, 2)), dma((3, 2)), dma((3, 2)),
            dma((3,)), dma((3,)), dma((3,)), dma((3,)),
        ],
        compiler_params=pltpu.CompilerParams(
            collective_id=0, has_side_effects=True, vmem_limit_bytes=48 << 20
        ),
        cost_estimate=pl.CostEstimate(
            flops=6 * TOK * ROWS * D, bytes_accessed=4 * TOK * D, transcendentals=TOK * ROWS
        ),
    )(hidden_states.T, embedding, targets.reshape(1, TOK), prior_lse.reshape(1, TOK))
    return loss.reshape(TOK), grad


def solution(mesh):
    placed = (P("dp", "tensor"), P(("dp", "tensor"), None), P("dp"), P("dp"))
    return jax.shard_map(
        body, mesh=mesh, in_specs=placed, out_specs=(P("dp"), P("dp", "tensor")), check_vma=False
    )
```

```python
import functools

import jax
import jax.numpy as jnp
from jax import lax
from jax.experimental import pallas as pl
from jax.experimental.pallas import tpu as pltpu
from jax.sharding import PartitionSpec as P

MESH = pl.DeviceIdType.MESH
BF16 = jnp.bfloat16
F32 = jnp.float32
NX, NY, NZ, NK = 4, 8, 8, 4
D = 5376
QUARTER = D // NK
MAIN = QUARTER // 128 * 128
REST = QUARTER - MAIN
PART_A = 768
WIDTHS = (PART_A, QUARTER - PART_A)
KEPT = 3
SPLIT = 19 * 128
TOK = 128
SET = TOK // NK
SUB = SET // 2
PIECE = 16
BLOCK = 8 * PIECE
ROWS = NY * NZ * PIECE


def device(x, y, z, c):
    return (((z % 2) * NX + x) * NY + y) * 2 + c, z // 2


def at_row(row):
    return pl.ds(pl.multiple_of(row * PIECE, PIECE), PIECE)


def ring_offset(m):
    return ((m + 1) // 2) * (1 - 2 * (m % 2))


def rearranged(quarters):
    return jnp.concatenate(
        [q[:, :MAIN] for q in quarters] + [q[:, MAIN:] for q in quarters], axis=1
    )


def kernel(
    hid_hbm, emb_hbm, tgt_hbm, pri_hbm, loss, out,
    hid, emb, tgt, pri, g, ebuf, hidn, hb, ht, lt, gl, raw, coef, meta, stat, lbuf,
    part_a, part_b, r1_a, r1_b, s2_a, s2_b, rd_a, rd_b, r3_a, r3_b, zs_a, zs_b, zr_a, zr_b,
    in_s, e_s, g_r, s_r, g_s, s_s, ha_s, ha_r, hx_s, hx_r,
    m_s, m_r, t_s, t_r, l_s, l_r, o_s, o_r, d_s, d_r, q_s, w_s, w_r, z_s, z_r,
):
    dp = lax.axis_index("dp")
    k = lax.axis_index("tensor")
    c = dp % 2
    y = dp // 2 % NY
    x = dp // (2 * NY) % NX
    zl = dp // (2 * NY * NX)
    z = 2 * k + zl

    def x_dev(d):
        return device((x + d) % NX, y, z, c)

    def k_dev(kk):
        return device(x, y, 2 * kk + zl, c)

    sibling = device(x, y, z, 1 - c)

    arguments = [
        pltpu.make_async_copy(src, dst, in_s.at[n])
        for n, (src, dst) in enumerate(((hid_hbm, hid), (emb_hbm, emb), (tgt_hbm, tgt), (pri_hbm, pri)))
    ]
    for argument in arguments:
        argument.start()

    partners = [sibling]
    partners += [device(x, (y + d) % NY, z, c) for d in (1, 2, 6, 7)]
    partners += [device(x, y, (z + d) % NZ, c) for d in (1, 2, 4, 6, 7)]
    partners += [x_dev(d) for d in (1, 2, 3)]
    barrier = pltpu.get_barrier_semaphore()
    for partner in partners:
        pl.semaphore_signal(barrier, inc=1, device_id=partner, device_id_type=MESH)

    for argument in arguments:
        argument.wait()
    for lo in range(0, QUARTER, 128):
        hi = min(lo + 128, QUARTER)
        hidn[:, lo:hi] = hid[lo:hi, :].astype(F32).T.astype(BF16)
    t = tgt[...]
    b = t // 8
    t_dp, t_k = b // 4, b % 4
    t_z = 2 * t_k + t_dp // (2 * NY * NX)
    place = (t_dp // (2 * NY) % NX) * ROWS + (t_z * NY + t_dp // 2 % NY) * PIECE + t_dp % 2 * 8 + t % 8
    meta[x] = jnp.concatenate([place.astype(F32), pri[...], jnp.zeros((6, TOK), F32)], axis=0)
    pl.semaphore_wait(barrier, len(partners))

    def received(ref, recv):
        copy(ref, ref, e_s.at[0], recv, sibling).wait_recv()

    def sent(ref, send):
        copy(ref, ref, send, e_s.at[1], sibling).wait_send()

    def copy(src, dst, send, recv, where):
        return pltpu.make_async_remote_copy(
            src_ref=src, dst_ref=dst, send_sem=send, recv_sem=recv,
            device_id=where, device_id_type=MESH,
        )

    e_copy = copy(emb, ebuf, e_s.at[0], e_s.at[1], sibling)
    e_copy.start()

    def set_rows(kk):
        return pl.ds(pl.multiple_of(kk * SET, SET), SET)

    def hidden_set(d):
        kk = (k + d) % NK
        return copy(hidn.at[set_rows(kk)], hb.at[x, k], ha_s.at[0], ha_r.at[d - 1], k_dev(kk))

    def hidden_x(j, d):
        ref = hb.at[x, j]
        return copy(ref, ref, hx_s.at[0], hx_r.at[0], x_dev(d))

    def hidden_on(d):
        received(hb.at[x, (k + NK - d) % NK], ha_r.at[d - 1])
        for e in (1, 3, 2):
            hidden_x((k + NK - d) % NK, e).start()

    def to_x(buf, send, recv, d):
        return copy(buf.at[x], buf.at[x], send.at[0], recv.at[0], x_dev(d))

    hb[x, k] = hidn[set_rows(k), :]
    e_copy.wait()
    mine, other = emb[...], ebuf[...]
    rows = jnp.concatenate(
        [jnp.where(c == 0, mine, other), jnp.where(c == 0, other, mine)], axis=0
    )
    g[at_row(z * NY + y), :] = rearranged(
        [rows[:, j * QUARTER:(j + 1) * QUARTER] for j in range(NK)]
    )

    def bring_in(h):
        outer, inner = (z, y) if h == 0 else (y, z)
        spans = (slice(0, SPLIT), slice(SPLIT, D))

        def number(o, i):
            return o * 8 + i if h == 0 else i * 8 + o

        def ring_dev(o, i):
            return device(x, i, o, c) if h == 0 else device(x, o, i, c)

        outer_next = ring_dev((outer + 1) % 8, inner)
        outer_last = ring_dev((outer + 7) % 8, inner)

        def piece(n, share):
            return g.at[at_row(n), spans[share]]

        def to_ring(o, i, where, recv):
            ref = piece(number(o, i), h)
            copy(ref, ref, g_s.at[0], g_r.at[recv], where).start()

        def to_inner(i, d, recv):
            to_ring(outer, i, ring_dev(outer, (inner + d + 8) % 8), recv)

        def to_sibling(o, i):
            ref = piece(number(o, i), h)
            copy(ref, ref, s_s.at[0], s_r.at[o], sibling).start()

        def to_outer(m):
            i = (inner + ring_offset(m) + 8) % 8
            to_ring(outer, i, outer_next, 8 + m)
            to_ring(outer, i, outer_last, 8 + m)

        for m, d in ((1, 1), (2, -1), (3, 2), (4, -2)):
            to_inner(inner, d, m)
        to_outer(0)
        for e in (1, 3, 2):
            hidden_x(k, e).start()
        for d in (1, 2, 3):
            to_x(meta, m_s, m_r, d).start()

        def first(m, onward):
            i = (inner + ring_offset(m) + 8) % 8
            received(piece(number(outer, i), h), g_r.at[m])
            for to, d in onward:
                to_inner(i, d, to)
            to_outer(m)
            to_sibling(outer, i)

        def second(ring, start, end):
            up, down = (outer + 8 - ring) % 8, (outer + ring) % 8

            def step(m, carry):
                i = (inner + ring_offset(m) + 8) % 8
                received(g.at[0:2 * PIECE, spans[h]], g_r.at[ring * 8 + m])
                to = (ring + 1) * 8 + m
                if ring == 3:
                    pl.when(m % 2 == 1)(lambda: to_ring(up, i, outer_next, to))
                    pl.when(m % 2 == 0)(lambda: to_ring(down, i, outer_last, to))
                else:
                    to_ring(up, i, outer_next, to)
                    to_ring(down, i, outer_last, to)
                to_sibling(up, i)
                to_sibling(down, i)
                return carry

            lax.fori_loop(start, end, step, 0)

        def logits(share, offsets):
            o0 = outer if share == h else inner
            by_z = share == 0
            starts = []
            for r in offsets:
                o = (o0 + r) % 8
                if by_z:
                    starts.append((pl.multiple_of(o * BLOCK, BLOCK), BLOCK))
                else:
                    starts += [(pl.multiple_of((i * 8 + o) * PIECE, PIECE), PIECE) for i in range(8)]
            left = jnp.concatenate([g[pl.ds(a, n), spans[share]] for a, n in starts], axis=0)
            value = lax.dot_general(
                left, ht[:, spans[share]], (((1,), (1,)), ((), ())), preferred_element_type=F32
            )
            at = 0
            for a, n in starts:
                lt[share, pl.ds(a, n), :] = value[at:at + n]
                at += n

        def await_sibling(r):
            rows = BLOCK - PIECE if isinstance(r, int) and r == 0 else BLOCK
            received(g.at[0:rows, spans[1 - h]], s_r.at[(inner + r) % 8])

        def schedule():
            for m, onward in ((1, ()), (2, ()), (3, ((5, 1), (7, 2))), (4, ((6, -1),))):
                first(m, onward)
            for d in (1, 3, 2):
                hidden_set(d).start()
            second(1, 0, 5)
            for m in (5, 6, 7):
                first(m, ())
            second(2, 0, 5)
            hidden_on(1)
            hidden_on(3)
            second(1, 5, 8)
            hidden_on(2)
            second(2, 5, 8)

        schedule()
        received(hb.at[0:NX - 1], hx_r.at[0])
        for xx in range(NX):
            ht[xx * SET:(xx + 1) * SET, :] = rearranged([hb[xx, j] for j in range(NK)])

        def early(r, carry):
            second(3, 4 * (r - 1), 4 * r)
            logits(h, (r, 8 - r))
            await_sibling(r)
            await_sibling(8 - r)
            logits(1 - h, (r, 8 - r))
            return carry

        lax.fori_loop(1, 3, early, 0)
        logits(h, (3, 5))
        logits(h, (0,))
        await_sibling(0)
        logits(1 - h, (0,))
        await_sibling(3)
        await_sibling(5)
        logits(1 - h, (3, 5))
        across = (outer + 4) % 8
        for m in range(8):
            i = (inner + ring_offset(m) + 8) % 8
            received(piece(number(across, i), h), g_r.at[32 + m])
            to_sibling(across, i)
        logits(h, (4,))
        await_sibling(4)
        logits(1 - h, (4,))

        sent(g.at[0:ROWS - PIECE, spans[h]], g_s.at[0])
        sent(g.at[0:ROWS - PIECE, spans[h]], s_s.at[0])

    for core in (0, 1):
        pl.when(c == core)(functools.partial(bring_in, core))

    lane_set = lax.broadcasted_iota(jnp.int32, (8, TOK), 1) // SET
    received(meta.at[0:NX - 1], m_r.at[0])
    info = jnp.zeros((8, TOK), F32)
    for xx in range(NX):
        turned = pltpu.roll(meta[xx], (xx + NX - k) % NX * SET, axis=1)
        info = jnp.where(lane_set == xx, turned, info)
    column = info[0:1] - (x * ROWS).astype(F32)
    owned = (column >= 0.0) & (column < float(ROWS))
    prior = info[1:2]

    peaks = jnp.full((8, TOK), -jnp.inf, F32)
    for n in range(8):
        span = slice(n * BLOCK, (n + 1) * BLOCK)
        value = lt[0, span, :] + lt[1, span, :]
        lt[0, span, :] = value
        peaks = jnp.maximum(peaks, jnp.max(value.reshape(BLOCK // 8, 8, TOK), axis=0))
    peak = jnp.max(peaks, axis=0, keepdims=True)
    total = jnp.zeros((8, TOK), F32)
    target = jnp.zeros((8, TOK), F32)
    row_id = lax.broadcasted_iota(jnp.int32, (BLOCK, TOK), 0).astype(F32)
    for n in range(8):
        span = slice(n * BLOCK, (n + 1) * BLOCK)
        value = lt[0, span, :]
        hit = row_id == column - float(n * BLOCK)
        power = jnp.exp(value - peak)
        lt[1, span, :] = jnp.where(hit, 0.0, power)
        total += jnp.sum(power.reshape(BLOCK // 8, 8, TOK), axis=0)
        target += jnp.sum(jnp.where(hit, value, 0.0).reshape(BLOCK // 8, 8, TOK), axis=0)
    my_target = jnp.sum(target, axis=0, keepdims=True)
    stat[x] = jnp.concatenate(
        [peak, jnp.sum(total, axis=0, keepdims=True), my_target, jnp.zeros((5, TOK), F32)], axis=0
    )
    for d in (1, 2, 3):
        to_x(stat, t_s, t_r, d).start()

    column_t = jnp.broadcast_to(column, (8, TOK)).T[:, 0:1]
    lane_id = lax.broadcasted_iota(jnp.int32, (TOK, BLOCK), 1).astype(F32)
    for n in range(8):
        span = slice(n * BLOCK, (n + 1) * BLOCK)
        gl[0:TOK, span] = lt[1, span, :].T.astype(BF16)
        gl[TOK:, span] = jnp.where(lane_id == column_t - float(n * BLOCK), 1.0, 0.0).astype(BF16)

    units = ((2, 1), (2, 0), (1, 0), (3, 0), (1, 1), (3, 1), (0, 0), (0, 1))
    turns = (2, 1, 3, 0)
    parts, r1s, s2s, rds = (part_a, part_b), (r1_a, r1_b), (s2_a, s2_b), (rd_a, rd_b)
    r3s, zss, zrs = (r3_a, r3_b), (zs_a, zs_b), (zr_a, zr_b)

    def place_of(u):
        turn, p = units[u]
        return turns.index(turn), p

    def products(u, use):
        turn, p = units[u]
        j = (k + turn) % NK
        for lo, hi in ((0, 512), (512, PART_A)) if p == 0 else ((PART_A, MAIN),):
            at = pl.ds(pl.multiple_of(j * MAIN + lo, 128), hi - lo)
            use(lo - p * PART_A, jnp.dot(gl[...], g[:, at], preferred_element_type=F32))
        if p == 1:
            at = pl.ds(pl.multiple_of(NK * MAIN + j // 2 * 128, 128), 128)
            value = jnp.dot(gl[...], g[:, at], preferred_element_type=F32)
            use(MAIN - PART_A, pltpu.roll(value, j % 2 * REST, axis=1)[:, :REST])

    def weigh(u):
        q, p = place_of(u)

        def use(lo, value):
            for at in range(0, value.shape[1], 128):
                w = min(128, value.shape[1] - at)
                mixed = (
                    value[:TOK, at:at + w] * coef[0, :, :w] + value[TOK:, at:at + w] * coef[1, :, :w]
                )
                parts[p][q, :, lo + at:lo + at + w] = mixed.astype(BF16)

        return use

    def keep(u):
        def use(lo, value):
            raw[u, :, lo:lo + value.shape[1]] = value

        return use

    for u in range(KEPT):
        products(u, keep(u))

    received(stat.at[0:NX - 1], t_r.at[0])
    top = prior
    for xx in range(NX):
        top = jnp.maximum(top, stat[xx, 0:1, :])
    whole = jnp.exp(prior - top)
    logit = jnp.zeros((1, TOK), F32)
    for xx in range(NX):
        whole += stat[xx, 1:2, :] * jnp.exp(stat[xx, 0:1, :] - top)
        logit += stat[xx, 2:3, :]
    lse = top + jnp.log(whole)
    weights = jnp.concatenate(
        [jnp.exp(peak - lse), jnp.where(owned, jnp.exp(my_target - lse) - 1.0, 0.0),
         jnp.zeros((6, TOK), F32)], axis=0,
    ).T
    coef[0] = jnp.broadcast_to(weights[:, 0:1], (TOK, 128))
    coef[1] = jnp.broadcast_to(weights[:, 1:2], (TOK, 128))

    def x_rows(d):
        return pl.ds(pl.multiple_of((x + d) % NX * SET, SET), SET)

    def x_half(d, way):
        return pl.ds(pl.multiple_of((x + d) % NX * SET + way * SUB, SUB), SUB)

    ways = ((0, 1, 3), (1, 3, 1))

    def opposite_copy(u, way, d):
        q, p = place_of(u)
        return copy(parts[p].at[q, x_half(2, way)], r1s[p].at[q, way], o_s.at[p], o_r.at[u], x_dev(d))

    def direct_copy(u, way, d):
        q, p = place_of(u)
        return copy(parts[p].at[q, x_half(d, way)], rds[p].at[q, way], d_s.at[p], d_r.at[u], x_dev(d))

    def sum_copy(u, way, d):
        q, p = place_of(u)
        return copy(s2s[p].at[q, way], rds[p].at[q, 2 + way], q_s.at[p], d_r.at[u], x_dev(d))

    def straight_copy(p, d):
        return copy(parts[p].at[3, x_rows(d)], r3s[p].at[d - 1], w_s.at[p], w_r.at[p], x_dev(d))

    def z_copy(u):
        q, p = place_of(u)
        return copy(zss[p].at[q], zrs[p].at[q], z_s.at[p], z_r.at[u], k_dev((k + units[u][0]) % NK))

    def send_first(u):
        q, p = place_of(u)
        if q == 3:
            for d in (2, 1, 3):
                straight_copy(p, d).start()
            return
        for way, near, _ in ways:
            opposite_copy(u, way, near).start()
        for way, _, far in ways:
            direct_copy(u, way, far).start()

    def multiply(u):
        if u < KEPT:
            width = WIDTHS[units[u][1]]
            for lo in range(0, width, 128):
                weigh(u)(lo, raw[u, :, lo:min(lo + 128, width)])
        else:
            products(u, weigh(u))
        send_first(u)

    def add_first(u):
        q, p = place_of(u)
        received(r1s[p].at[q], o_r.at[u])
        for way, near, _ in ways:
            s2s[p][q, way] = (
                parts[p][q, x_half(near, way), :].astype(F32) + r1s[p][q, way].astype(F32)
            ).astype(BF16)
            sum_copy(u, way, near).start()

    def add_last(u):
        q, p = place_of(u)
        received(rds[p].at[q], d_r.at[u])
        for way in (0, 1):
            zss[p][q, way * SUB:(way + 1) * SUB, :] = (
                parts[p][q, x_half(0, way), :].astype(F32)
                + rds[p][q, way].astype(F32) + rds[p][q, 2 + way].astype(F32)
            ).astype(BF16)
        z_copy(u).start()

    def own(p):
        received(r3s[p], w_r.at[p])
        value = parts[p][3, x_rows(0), :].astype(F32)
        for d in (1, 2, 3):
            value += r3s[p][d - 1].astype(F32)
        out[set_rows(k), p * PART_A:p * PART_A + WIDTHS[p]] = value.astype(BF16)

    def finish(u):
        q, p = place_of(u)
        received(zrs[p].at[q], z_r.at[u])
        rows = set_rows((k + NK - units[u][0]) % NK)
        out[rows, p * PART_A:p * PART_A + WIDTHS[p]] = zrs[p][q]

    multiply(0)
    lbuf[k] = jnp.broadcast_to(lse - logit, (8, TOK))

    def loss_to(d):
        return copy(lbuf.at[k], lbuf.at[k], l_s.at[0], l_r.at[0], k_dev((k + d) % NK))

    for d in (1, 2, 3):
        loss_to(d).start()
    multiply(1)
    multiply(2)
    multiply(3)
    add_first(0)
    multiply(4)
    add_first(1)
    multiply(5)
    add_first(2)
    add_first(3)
    add_last(0)
    add_first(4)
    add_last(1)
    add_first(5)
    multiply(6)
    add_last(2)
    multiply(7)
    add_last(3)
    add_last(4)
    add_last(5)

    received(lbuf.at[0:NK - 1], l_r.at[0])
    result = jnp.zeros((8, TOK), F32)
    for kk in range(NK):
        turned = pltpu.roll(lbuf[kk], (kk + NX - x) % NX * SET, axis=1)
        result = jnp.where(lane_set == kk, turned, result)
    loss[...] = result[0:1]

    finish(0)
    finish(1)
    own(0)
    own(1)
    for u in (2, 4, 3, 5):
        finish(u)

    sent(hidn.at[0:TOK - SET], ha_s.at[0])
    sent(hb.at[0:NX - 1], hx_s.at[0])
    for buf, send in ((meta, m_s), (stat, t_s), (lbuf, l_s)):
        sent(buf.at[0:3], send.at[0])
    for p in (0, 1):
        sent(r1s[p], o_s.at[p])
        sent(r1s[p], d_s.at[p])
        sent(r1s[p], q_s.at[p])
        sent(r3s[p], w_s.at[p])
        sent(zss[p], z_s.at[p])


def body(hidden_states, embedding, targets, prior_lse):
    dma = pltpu.SemaphoreType.DMA
    hbm = pl.BlockSpec(memory_space=pltpu.HBM)
    vmem = pl.BlockSpec(memory_space=pltpu.VMEM)
    arguments = (hidden_states.T, embedding, targets.reshape(1, TOK), prior_lse.reshape(1, TOK))
    pair = [(WIDTHS[0],), (WIDTHS[1],)]
    loss, grad = pl.pallas_call(
        kernel,
        out_shape=(
            jax.ShapeDtypeStruct((1, TOK), F32),
            jax.ShapeDtypeStruct((TOK, QUARTER), BF16),
        ),
        in_specs=[hbm] * 4,
        out_specs=(vmem, vmem),
        scratch_shapes=[
            pltpu.VMEM((QUARTER, TOK), BF16),
            pltpu.VMEM((8, D), BF16),
            pltpu.VMEM((1, TOK), jnp.int32),
            pltpu.VMEM((1, TOK), F32),
            pltpu.VMEM((ROWS, D), BF16),
            pltpu.VMEM((8, D), BF16),
            pltpu.VMEM((TOK, QUARTER), BF16),
            pltpu.VMEM((NX, NK, SET, QUARTER), BF16),
            pltpu.VMEM((TOK, D), BF16),
            pltpu.VMEM((2, ROWS, TOK), F32),
            pltpu.VMEM((2 * TOK, ROWS), BF16),
            pltpu.VMEM((KEPT, 2 * TOK, WIDTHS[0]), F32),
            pltpu.VMEM((2, TOK, 128), F32),
            pltpu.VMEM((NX, 8, TOK), F32),
            pltpu.VMEM((NX, 8, TOK), F32),
            pltpu.VMEM((NK, 8, TOK), F32),
            *[pltpu.VMEM((NK, TOK) + w, BF16) for w in pair],
            *[pltpu.VMEM((NK - 1, 2, SUB) + w, BF16) for w in pair * 2],
            *[pltpu.VMEM((NK - 1, 4, SUB) + w, BF16) for w in pair],
            *[pltpu.VMEM((NX - 1, SET) + w, BF16) for w in pair],
            *[pltpu.VMEM((NK - 1, SET) + w, BF16) for w in pair * 2],
            *[dma((n,)) for n in (4, 2, 40, 8, 1, 1, 1, 3, 1, 1)],
            *[dma((n,)) for n in (1, 1, 1, 1, 1, 1, 2, 6, 2, 6, 2, 2, 2, 2, 6)],
        ],
        compiler_params=pltpu.CompilerParams(
            collective_id=0, has_side_effects=True, vmem_limit_bytes=48 << 20
        ),
        cost_estimate=pl.CostEstimate(
            flops=6 * TOK * ROWS * D, bytes_accessed=4 * TOK * D, transcendentals=TOK * ROWS
        ),
    )(*[pltpu.with_memory_space_constraint(a, pltpu.HBM) for a in arguments])
    return loss.reshape(TOK), grad


def solution(mesh):
    placed = (P("dp", "tensor"), P(("dp", "tensor"), None), P("dp"), P("dp"))
    return jax.shard_map(
        body, mesh=mesh, in_specs=placed, out_specs=(P("dp"), P("dp", "tensor")), check_vma=False
    )
```

```python
import functools

import jax
import jax.numpy as jnp
from jax import lax
from jax.experimental import pallas as pl
from jax.experimental.pallas import tpu as pltpu
from jax.sharding import PartitionSpec as P

MESH = pl.DeviceIdType.MESH
BF16 = jnp.bfloat16
F32 = jnp.float32
NX, NY, NZ, NK = 4, 8, 8, 4
D = 5376
QUARTER = D // NK
MAIN = QUARTER // 128 * 128
REST = QUARTER - MAIN
PART_A = 768
WIDTHS = (PART_A, QUARTER - PART_A)
KEPT = 3
SPLIT = 19 * 128
TOK = 128
SET = TOK // NK
SUB = SET // 2
PIECE = 16
BLOCK = 8 * PIECE
ROWS = NY * NZ * PIECE


STEPS = (
    (
        ("send", 1), ("send", 3), ("send", 2), ("first", 1, 8, False), ("outer", 0), ("outer", 1),
        ("outer", 2), ("outer", 3), ("outer", 4), ("outer", 5), ("outer", 6), ("outer", 7),
        ("pass", 1), ("pass", 3), ("pass", 2), ("second", 1, 0, 8), ("second", 2, 0, 5),
        ("features",), ("own", 0), ("sibling", 0), ("second", 2, 5, 8), ("own", 1),
        ("second", 3, 0, 4), ("sibling", 1), ("own", 2), ("second", 3, 4, 8), ("sibling", 2),
        ("own", 3), ("sibling", 3), ("opposite",), ("own", 4), ("sibling", 4),
    ),
    (
        ("outer", 0), ("send", 1), ("send", 3), ("send", 2), ("first", 1, 5, True),
        ("second", 1, 0, 5), ("first", 5, 8, True), ("pass", 1), ("pass", 3), ("pass", 2),
        ("second", 2, 0, 5), ("second", 1, 5, 8), ("features",), ("own", 0), ("sibling", 0),
        ("own", 1), ("second", 2, 5, 8), ("second", 3, 0, 4), ("sibling", 1), ("own", 2),
        ("second", 3, 4, 8), ("sibling", 2), ("own", 3), ("sibling", 3), ("opposite",), ("own", 4),
        ("sibling", 4),
    ),
)


def device(x, y, z, c):
    return (((z % 2) * NX + x) * NY + y) * 2 + c, z // 2


def at_row(row):
    return pl.ds(pl.multiple_of(row * PIECE, PIECE), PIECE)


def ring_offset(m):
    return ((m + 1) // 2) * (1 - 2 * (m % 2))


def rearranged(quarters):
    return jnp.concatenate(
        [q[:, :MAIN] for q in quarters] + [q[:, MAIN:] for q in quarters], axis=1
    )


def kernel(
    hid_hbm, emb_hbm, tgt_hbm, pri_hbm, loss, out,
    hid, emb, tgt, pri, g, ebuf, hidn, hb, ht, lt, gl, raw, coef, meta, stat, lbuf,
    part_a, part_b, r1_a, r1_b, s2_a, s2_b, rd_a, rd_b, r3_a, r3_b, zs_a, zs_b, zr_a, zr_b,
    in_s, e_s, g_r, s_r, g_s, s_s, ha_s, ha_r, hx_s, hx_r,
    m_s, m_r, t_s, t_r, l_s, l_r, o_s, o_r, d_s, d_r, q_s, w_s, w_r, z_s, z_r,
):
    dp = lax.axis_index("dp")
    k = lax.axis_index("tensor")
    c = dp % 2
    y = dp // 2 % NY
    x = dp // (2 * NY) % NX
    zl = dp // (2 * NY * NX)
    z = 2 * k + zl

    def x_dev(d):
        return device((x + d) % NX, y, z, c)

    def k_dev(kk):
        return device(x, y, 2 * kk + zl, c)

    sibling = device(x, y, z, 1 - c)

    arguments = [
        pltpu.make_async_copy(src, dst, in_s.at[n])
        for n, (src, dst) in enumerate(((hid_hbm, hid), (emb_hbm, emb), (tgt_hbm, tgt), (pri_hbm, pri)))
    ]
    for argument in arguments:
        argument.start()

    partners = [sibling]
    partners += [device(x, (y + d) % NY, z, c) for d in (1, 2, 6, 7)]
    partners += [device(x, y, (z + d) % NZ, c) for d in (1, 2, 4, 6, 7)]
    partners += [x_dev(d) for d in (1, 2, 3)]
    barrier = pltpu.get_barrier_semaphore()
    for partner in partners:
        pl.semaphore_signal(barrier, inc=1, device_id=partner, device_id_type=MESH)

    for argument in arguments:
        argument.wait()
    for lo in range(0, QUARTER, 128):
        hi = min(lo + 128, QUARTER)
        hidn[:, lo:hi] = hid[lo:hi, :].astype(F32).T.astype(BF16)
    t = tgt[...]
    b = t // 8
    t_dp, t_k = b // 4, b % 4
    t_z = 2 * t_k + t_dp // (2 * NY * NX)
    place = (t_dp // (2 * NY) % NX) * ROWS + (t_z * NY + t_dp // 2 % NY) * PIECE + t_dp % 2 * 8 + t % 8
    meta[x] = jnp.concatenate([place.astype(F32), pri[...], jnp.zeros((6, TOK), F32)], axis=0)
    pl.semaphore_wait(barrier, len(partners))

    def received(ref, recv):
        copy(ref, ref, e_s.at[0], recv, sibling).wait_recv()

    def sent(ref, send):
        copy(ref, ref, send, e_s.at[1], sibling).wait_send()

    def copy(src, dst, send, recv, where):
        return pltpu.make_async_remote_copy(
            src_ref=src, dst_ref=dst, send_sem=send, recv_sem=recv,
            device_id=where, device_id_type=MESH,
        )

    e_copy = copy(emb, ebuf, e_s.at[0], e_s.at[1], sibling)
    e_copy.start()

    def set_rows(kk):
        return pl.ds(pl.multiple_of(kk * SET, SET), SET)

    def hidden_set(d):
        kk = (k + d) % NK
        return copy(hidn.at[set_rows(kk)], hb.at[x, k], ha_s.at[0], ha_r.at[d - 1], k_dev(kk))

    def hidden_x(j, d):
        ref = hb.at[x, j]
        return copy(ref, ref, hx_s.at[0], hx_r.at[0], x_dev(d))

    def hidden_on(d):
        received(hb.at[x, (k + NK - d) % NK], ha_r.at[d - 1])
        for e in (1, 3, 2):
            hidden_x((k + NK - d) % NK, e).start()

    def to_x(buf, send, recv, d):
        return copy(buf.at[x], buf.at[x], send.at[0], recv.at[0], x_dev(d))

    hb[x, k] = hidn[set_rows(k), :]
    e_copy.wait()
    mine, other = emb[...], ebuf[...]
    rows = jnp.concatenate(
        [jnp.where(c == 0, mine, other), jnp.where(c == 0, other, mine)], axis=0
    )
    g[at_row(z * NY + y), :] = rearranged(
        [rows[:, j * QUARTER:(j + 1) * QUARTER] for j in range(NK)]
    )

    def bring_in(h):
        outer, inner = (z, y) if h == 0 else (y, z)
        spans = (slice(0, SPLIT), slice(SPLIT, D))

        def number(o, i):
            return o * 8 + i if h == 0 else i * 8 + o

        def ring_dev(o, i):
            return device(x, i, o, c) if h == 0 else device(x, o, i, c)

        outer_next = ring_dev((outer + 1) % 8, inner)
        outer_last = ring_dev((outer + 7) % 8, inner)

        def piece(n, share):
            return g.at[at_row(n), spans[share]]

        def to_ring(o, i, where, recv):
            ref = piece(number(o, i), h)
            copy(ref, ref, g_s.at[0], g_r.at[recv], where).start()

        def to_inner(i, d, recv):
            to_ring(outer, i, ring_dev(outer, (inner + d + 8) % 8), recv)

        def to_sibling(o, i):
            ref = piece(number(o, i), h)
            copy(ref, ref, s_s.at[0], s_r.at[o], sibling).start()

        def to_outer(m):
            i = (inner + ring_offset(m) + 8) % 8
            to_ring(outer, i, outer_next, 8 + m)
            to_ring(outer, i, outer_last, 8 + m)

        for m, d in ((1, 1), (2, -1), (3, 2), (4, -2)):
            to_inner(inner, d, m)
        for e in (1, 3, 2):
            hidden_x(k, e).start()
        for d in (1, 2, 3):
            to_x(meta, m_s, m_r, d).start()

        def first(start, end, outward):
            for m in range(start, end):
                i = (inner + ring_offset(m) + 8) % 8
                received(piece(number(outer, i), h), g_r.at[m])
                for to, d in {3: ((5, 1), (7, 2)), 4: ((6, -1),)}.get(m, ()):
                    to_inner(i, d, to)
                if outward:
                    to_outer(m)
                to_sibling(outer, i)

        def second(ring, start, end):
            up, down = (outer + 8 - ring) % 8, (outer + ring) % 8

            def step(m, carry):
                i = (inner + ring_offset(m) + 8) % 8
                received(g.at[0:2 * PIECE, spans[h]], g_r.at[ring * 8 + m])
                to = (ring + 1) * 8 + m
                if ring == 3:
                    pl.when(m % 2 == 1)(lambda: to_ring(up, i, outer_next, to))
                    pl.when(m % 2 == 0)(lambda: to_ring(down, i, outer_last, to))
                else:
                    to_ring(up, i, outer_next, to)
                    to_ring(down, i, outer_last, to)
                to_sibling(up, i)
                to_sibling(down, i)
                return carry

            lax.fori_loop(start, end, step, 0)

        def logits(share, offsets):
            o0 = outer if share == h else inner
            by_z = share == 0
            starts = []
            for r in offsets:
                o = (o0 + r) % 8
                if by_z:
                    starts.append((pl.multiple_of(o * BLOCK, BLOCK), BLOCK))
                else:
                    starts += [(pl.multiple_of((i * 8 + o) * PIECE, PIECE), PIECE) for i in range(8)]
            left = jnp.concatenate([g[pl.ds(a, n), spans[share]] for a, n in starts], axis=0)
            value = lax.dot_general(
                left, ht[:, spans[share]], (((1,), (1,)), ((), ())), preferred_element_type=F32
            )
            at = 0
            for a, n in starts:
                lt[share, pl.ds(a, n), :] = value[at:at + n]
                at += n

        def await_sibling(r):
            rows = BLOCK - PIECE if isinstance(r, int) and r == 0 else BLOCK
            received(g.at[0:rows, spans[1 - h]], s_r.at[(inner + r) % 8])

        def features():
            received(hb.at[0:NX - 1], hx_r.at[0])
            for xx in range(NX):
                ht[xx * SET:(xx + 1) * SET, :] = rearranged([hb[xx, j] for j in range(NK)])

        def own_logits(r):
            logits(h, (r,) if r % 4 == 0 else (r, 8 - r))

        def sibling_logits(r):
            for b in (r,) if r % 4 == 0 else (r, 8 - r):
                await_sibling(b)
            logits(1 - h, (r,) if r % 4 == 0 else (r, 8 - r))

        def opposite():
            across = (outer + 4) % 8
            for m in range(8):
                i = (inner + ring_offset(m) + 8) % 8
                received(piece(number(across, i), h), g_r.at[32 + m])
                to_sibling(across, i)

        acts = {
            "first": first, "outer": to_outer, "second": second, "opposite": opposite,
            "send": lambda d: hidden_set(d).start(), "pass": hidden_on, "features": features,
            "own": own_logits, "sibling": sibling_logits,
        }
        for act, *numbers in STEPS[h]:
            acts[act](*numbers)

        sent(g.at[0:ROWS - PIECE, spans[h]], g_s.at[0])
        sent(g.at[0:ROWS - PIECE, spans[h]], s_s.at[0])

    for core in (0, 1):
        pl.when(c == core)(functools.partial(bring_in, core))

    lane_set = lax.broadcasted_iota(jnp.int32, (8, TOK), 1) // SET
    received(meta.at[0:NX - 1], m_r.at[0])
    info = jnp.zeros((8, TOK), F32)
    for xx in range(NX):
        turned = pltpu.roll(meta[xx], (xx + NX - k) % NX * SET, axis=1)
        info = jnp.where(lane_set == xx, turned, info)
    column = info[0:1] - (x * ROWS).astype(F32)
    owned = (column >= 0.0) & (column < float(ROWS))
    prior = info[1:2]

    peaks = jnp.full((8, TOK), -jnp.inf, F32)
    for n in range(8):
        span = slice(n * BLOCK, (n + 1) * BLOCK)
        value = lt[0, span, :] + lt[1, span, :]
        lt[0, span, :] = value
        peaks = jnp.maximum(peaks, jnp.max(value.reshape(BLOCK // 8, 8, TOK), axis=0))
    peak = jnp.max(peaks, axis=0, keepdims=True)
    total = jnp.zeros((8, TOK), F32)
    target = jnp.zeros((8, TOK), F32)
    row_id = lax.broadcasted_iota(jnp.int32, (BLOCK, TOK), 0).astype(F32)
    for n in range(8):
        span = slice(n * BLOCK, (n + 1) * BLOCK)
        value = lt[0, span, :]
        hit = row_id == column - float(n * BLOCK)
        power = jnp.exp(value - peak)
        lt[1, span, :] = jnp.where(hit, 0.0, power)
        total += jnp.sum(power.reshape(BLOCK // 8, 8, TOK), axis=0)
        target += jnp.sum(jnp.where(hit, value, 0.0).reshape(BLOCK // 8, 8, TOK), axis=0)
    my_target = jnp.sum(target, axis=0, keepdims=True)
    stat[x] = jnp.concatenate(
        [peak, jnp.sum(total, axis=0, keepdims=True), my_target, jnp.zeros((5, TOK), F32)], axis=0
    )
    for d in (1, 2, 3):
        to_x(stat, t_s, t_r, d).start()

    column_t = jnp.broadcast_to(column, (8, TOK)).T[:, 0:1]
    lane_id = lax.broadcasted_iota(jnp.int32, (TOK, BLOCK), 1).astype(F32)
    for n in range(8):
        span = slice(n * BLOCK, (n + 1) * BLOCK)
        gl[0:TOK, span] = lt[1, span, :].T.astype(BF16)
        gl[TOK:, span] = jnp.where(lane_id == column_t - float(n * BLOCK), 1.0, 0.0).astype(BF16)

    units = ((2, 1), (2, 0), (1, 0), (3, 0), (1, 1), (3, 1), (0, 0), (0, 1))
    turns = (2, 1, 3, 0)
    parts, r1s, s2s, rds = (part_a, part_b), (r1_a, r1_b), (s2_a, s2_b), (rd_a, rd_b)
    r3s, zss, zrs = (r3_a, r3_b), (zs_a, zs_b), (zr_a, zr_b)

    def place_of(u):
        turn, p = units[u]
        return turns.index(turn), p

    def products(u, use):
        turn, p = units[u]
        j = (k + turn) % NK
        for lo, hi in ((0, 512), (512, PART_A)) if p == 0 else ((PART_A, MAIN),):
            at = pl.ds(pl.multiple_of(j * MAIN + lo, 128), hi - lo)
            use(lo - p * PART_A, jnp.dot(gl[...], g[:, at], preferred_element_type=F32))
        if p == 1:
            at = pl.ds(pl.multiple_of(NK * MAIN + j // 2 * 128, 128), 128)
            value = jnp.dot(gl[...], g[:, at], preferred_element_type=F32)
            use(MAIN - PART_A, pltpu.roll(value, j % 2 * REST, axis=1)[:, :REST])

    def weigh(u):
        q, p = place_of(u)

        def use(lo, value):
            for at in range(0, value.shape[1], 128):
                w = min(128, value.shape[1] - at)
                mixed = (
                    value[:TOK, at:at + w] * coef[0, :, :w] + value[TOK:, at:at + w] * coef[1, :, :w]
                )
                parts[p][q, :, lo + at:lo + at + w] = mixed.astype(BF16)

        return use

    def keep(u):
        def use(lo, value):
            raw[u, :, lo:lo + value.shape[1]] = value

        return use

    for u in range(KEPT):
        products(u, keep(u))

    received(stat.at[0:NX - 1], t_r.at[0])
    top = prior
    for xx in range(NX):
        top = jnp.maximum(top, stat[xx, 0:1, :])
    whole = jnp.exp(prior - top)
    logit = jnp.zeros((1, TOK), F32)
    for xx in range(NX):
        whole += stat[xx, 1:2, :] * jnp.exp(stat[xx, 0:1, :] - top)
        logit += stat[xx, 2:3, :]
    lse = top + jnp.log(whole)
    weights = jnp.concatenate(
        [jnp.exp(peak - lse), jnp.where(owned, jnp.exp(my_target - lse) - 1.0, 0.0),
         jnp.zeros((6, TOK), F32)], axis=0,
    ).T
    coef[0] = jnp.broadcast_to(weights[:, 0:1], (TOK, 128))
    coef[1] = jnp.broadcast_to(weights[:, 1:2], (TOK, 128))

    def x_rows(d):
        return pl.ds(pl.multiple_of((x + d) % NX * SET, SET), SET)

    def x_half(d, way):
        return pl.ds(pl.multiple_of((x + d) % NX * SET + way * SUB, SUB), SUB)

    ways = ((0, 1, 3), (1, 3, 1))

    def opposite_copy(u, way, d):
        q, p = place_of(u)
        return copy(parts[p].at[q, x_half(2, way)], r1s[p].at[q, way], o_s.at[p], o_r.at[u], x_dev(d))

    def direct_copy(u, way, d):
        q, p = place_of(u)
        return copy(parts[p].at[q, x_half(d, way)], rds[p].at[q, way], d_s.at[p], d_r.at[u], x_dev(d))

    def sum_copy(u, way, d):
        q, p = place_of(u)
        return copy(s2s[p].at[q, way], rds[p].at[q, 2 + way], q_s.at[p], d_r.at[u], x_dev(d))

    def straight_copy(p, d):
        return copy(parts[p].at[3, x_rows(d)], r3s[p].at[d - 1], w_s.at[p], w_r.at[p], x_dev(d))

    def z_copy(u):
        q, p = place_of(u)
        return copy(zss[p].at[q], zrs[p].at[q], z_s.at[p], z_r.at[u], k_dev((k + units[u][0]) % NK))

    def send_first(u):
        q, p = place_of(u)
        if q == 3:
            for d in (2, 1, 3):
                straight_copy(p, d).start()
            return
        for way, near, _ in ways:
            opposite_copy(u, way, near).start()
        for way, _, far in ways:
            direct_copy(u, way, far).start()

    def multiply(u):
        if u < KEPT:
            width = WIDTHS[units[u][1]]
            for lo in range(0, width, 128):
                weigh(u)(lo, raw[u, :, lo:min(lo + 128, width)])
        else:
            products(u, weigh(u))
        send_first(u)

    def add_first(u):
        q, p = place_of(u)
        received(r1s[p].at[q], o_r.at[u])
        for way, near, _ in ways:
            s2s[p][q, way] = (
                parts[p][q, x_half(near, way), :].astype(F32) + r1s[p][q, way].astype(F32)
            ).astype(BF16)
            sum_copy(u, way, near).start()

    def add_last(u):
        q, p = place_of(u)
        received(rds[p].at[q], d_r.at[u])
        for way in (0, 1):
            zss[p][q, way * SUB:(way + 1) * SUB, :] = (
                parts[p][q, x_half(0, way), :].astype(F32)
                + rds[p][q, way].astype(F32) + rds[p][q, 2 + way].astype(F32)
            ).astype(BF16)
        z_copy(u).start()

    def own(p):
        received(r3s[p], w_r.at[p])
        value = parts[p][3, x_rows(0), :].astype(F32)
        for d in (1, 2, 3):
            value += r3s[p][d - 1].astype(F32)
        out[set_rows(k), p * PART_A:p * PART_A + WIDTHS[p]] = value.astype(BF16)

    def finish(u):
        q, p = place_of(u)
        received(zrs[p].at[q], z_r.at[u])
        rows = set_rows((k + NK - units[u][0]) % NK)
        out[rows, p * PART_A:p * PART_A + WIDTHS[p]] = zrs[p][q]

    multiply(0)
    lbuf[k] = jnp.broadcast_to(lse - logit, (8, TOK))

    def loss_to(d):
        return copy(lbuf.at[k], lbuf.at[k], l_s.at[0], l_r.at[0], k_dev((k + d) % NK))

    for d in (1, 2, 3):
        loss_to(d).start()
    multiply(1)
    multiply(2)
    multiply(3)
    add_first(0)
    multiply(4)
    add_first(1)
    multiply(5)
    add_first(2)
    add_first(3)
    add_last(0)
    add_first(4)
    add_last(1)
    add_first(5)
    add_last(2)
    add_last(3)
    multiply(6)
    add_last(4)
    add_last(5)
    multiply(7)

    received(lbuf.at[0:NK - 1], l_r.at[0])
    result = jnp.zeros((8, TOK), F32)
    for kk in range(NK):
        turned = pltpu.roll(lbuf[kk], (kk + NX - x) % NX * SET, axis=1)
        result = jnp.where(lane_set == kk, turned, result)
    loss[...] = result[0:1]

    finish(0)
    finish(1)
    own(0)
    own(1)
    for u in (2, 4, 3, 5):
        finish(u)

    sent(hidn.at[0:TOK - SET], ha_s.at[0])
    sent(hb.at[0:NX - 1], hx_s.at[0])
    for buf, send in ((meta, m_s), (stat, t_s), (lbuf, l_s)):
        sent(buf.at[0:3], send.at[0])
    for p in (0, 1):
        sent(r1s[p], o_s.at[p])
        sent(r1s[p], d_s.at[p])
        sent(r1s[p], q_s.at[p])
        sent(r3s[p], w_s.at[p])
        sent(zss[p], z_s.at[p])


def body(hidden_states, embedding, targets, prior_lse):
    dma = pltpu.SemaphoreType.DMA
    hbm = pl.BlockSpec(memory_space=pltpu.HBM)
    vmem = pl.BlockSpec(memory_space=pltpu.VMEM)
    arguments = (hidden_states.T, embedding, targets.reshape(1, TOK), prior_lse.reshape(1, TOK))
    pair = [(WIDTHS[0],), (WIDTHS[1],)]
    loss, grad = pl.pallas_call(
        kernel,
        out_shape=(
            jax.ShapeDtypeStruct((1, TOK), F32),
            jax.ShapeDtypeStruct((TOK, QUARTER), BF16),
        ),
        in_specs=[hbm] * 4,
        out_specs=(vmem, vmem),
        scratch_shapes=[
            pltpu.VMEM((QUARTER, TOK), BF16),
            pltpu.VMEM((8, D), BF16),
            pltpu.VMEM((1, TOK), jnp.int32),
            pltpu.VMEM((1, TOK), F32),
            pltpu.VMEM((ROWS, D), BF16),
            pltpu.VMEM((8, D), BF16),
            pltpu.VMEM((TOK, QUARTER), BF16),
            pltpu.VMEM((NX, NK, SET, QUARTER), BF16),
            pltpu.VMEM((TOK, D), BF16),
            pltpu.VMEM((2, ROWS, TOK), F32),
            pltpu.VMEM((2 * TOK, ROWS), BF16),
            pltpu.VMEM((KEPT, 2 * TOK, WIDTHS[0]), F32),
            pltpu.VMEM((2, TOK, 128), F32),
            pltpu.VMEM((NX, 8, TOK), F32),
            pltpu.VMEM((NX, 8, TOK), F32),
            pltpu.VMEM((NK, 8, TOK), F32),
            *[pltpu.VMEM((NK, TOK) + w, BF16) for w in pair],
            *[pltpu.VMEM((NK - 1, 2, SUB) + w, BF16) for w in pair * 2],
            *[pltpu.VMEM((NK - 1, 4, SUB) + w, BF16) for w in pair],
            *[pltpu.VMEM((NX - 1, SET) + w, BF16) for w in pair],
            *[pltpu.VMEM((NK - 1, SET) + w, BF16) for w in pair * 2],
            *[dma((n,)) for n in (4, 2, 40, 8, 1, 1, 1, 3, 1, 1)],
            *[dma((n,)) for n in (1, 1, 1, 1, 1, 1, 2, 6, 2, 6, 2, 2, 2, 2, 6)],
        ],
        compiler_params=pltpu.CompilerParams(
            collective_id=0, has_side_effects=True, vmem_limit_bytes=48 << 20
        ),
        cost_estimate=pl.CostEstimate(
            flops=6 * TOK * ROWS * D, bytes_accessed=4 * TOK * D, transcendentals=TOK * ROWS
        ),
    )(*[pltpu.with_memory_space_constraint(a, pltpu.HBM) for a in arguments])
    return loss.reshape(TOK), grad


def solution(mesh):
    placed = (P("dp", "tensor"), P(("dp", "tensor"), None), P("dp"), P("dp"))
    return jax.shard_map(
        body, mesh=mesh, in_specs=placed, out_specs=(P("dp"), P("dp", "tensor")), check_vma=False
    )
```

```python
import functools

import jax
import jax.numpy as jnp
from jax import lax
from jax.experimental import pallas as pl
from jax.experimental.pallas import tpu as pltpu
from jax.sharding import PartitionSpec as P

MESH = pl.DeviceIdType.MESH
BF16 = jnp.bfloat16
F32 = jnp.float32
NX, NY, NZ, NK = 4, 8, 8, 4
D = 5376
QUARTER = D // NK
MAIN = QUARTER // 128 * 128
REST = QUARTER - MAIN
PART_A = 768
WIDTHS = (PART_A, QUARTER - PART_A)
KEPT = 5
SPLIT = 19 * 128
TOK = 128
SET = TOK // NK
SUB = SET // 2
PIECE = 16
BLOCK = 8 * PIECE
ROWS = NY * NZ * PIECE


STEPS = (
    (
        ("send", 1), ("send", 3), ("send", 2), ("first", 1, 3, False), ("outer", 0), ("outer", 1),
        ("first", 3, 8, False), ("pass", 1), ("pass", 3), ("pass", 2), ("outer", 2), ("outer", 3),
        ("outer", 4), ("second", 1, 0, 1), ("outer", 5), ("outer", 6), ("outer", 7),
        ("second", 1, 1, 8), ("second", 2, 0, 5), ("features",), ("own", 0), ("sibling", 0),
        ("second", 2, 5, 8), ("own", 1), ("second", 3, 0, 4), ("sibling", 1), ("own", 2),
        ("second", 3, 4, 8), ("sibling", 2), ("own", 3), ("sibling", 3), ("opposite",), ("own", 4),
        ("sibling", 4),
    ),
    (
        ("outer", 0), ("send", 1), ("send", 3), ("send", 2), ("second", 1, 0, 1),
        ("second", 2, 0, 1), ("first", 1, 5, True), ("pass", 1), ("pass", 3), ("pass", 2),
        ("second", 1, 1, 5), ("first", 5, 8, True), ("second", 2, 1, 5), ("second", 1, 5, 8),
        ("features",), ("own", 0), ("sibling", 0), ("own", 1), ("second", 2, 5, 8),
        ("second", 3, 0, 4), ("sibling", 1), ("own", 2), ("second", 3, 4, 8), ("sibling", 2),
        ("own", 3), ("sibling", 3), ("opposite",), ("own", 4), ("sibling", 4),
    ),
)


def device(x, y, z, c):
    return (((z % 2) * NX + x) * NY + y) * 2 + c, z // 2


def at_row(row):
    return pl.ds(pl.multiple_of(row * PIECE, PIECE), PIECE)


def ring_offset(m):
    return ((m + 1) // 2) * (1 - 2 * (m % 2))


def rearranged(quarters):
    return jnp.concatenate(
        [q[:, :MAIN] for q in quarters] + [q[:, MAIN:] for q in quarters], axis=1
    )


def kernel(
    hid_hbm, emb_hbm, tgt_hbm, pri_hbm, loss, out,
    hid, emb, tgt, pri, g, ebuf, hidn, hb, ht, lt, gl, raw, coef, meta, stat, lbuf,
    part_a, part_b, r1_a, r1_b, s2_a, s2_b, rd_a, rd_b, r3_a, r3_b, zs_a, zs_b, zr_a, zr_b,
    in_s, e_s, g_r, s_r, g_s, s_s, ha_s, ha_r, hx_s, hx_r,
    m_s, m_r, t_s, t_r, l_s, l_r, o_s, o_r, d_s, d_r, q_s, w_s, w_r, z_s, z_r,
):
    dp = lax.axis_index("dp")
    k = lax.axis_index("tensor")
    c = dp % 2
    y = dp // 2 % NY
    x = dp // (2 * NY) % NX
    zl = dp // (2 * NY * NX)
    z = 2 * k + zl

    def x_dev(d):
        return device((x + d) % NX, y, z, c)

    def k_dev(kk):
        return device(x, y, 2 * kk + zl, c)

    sibling = device(x, y, z, 1 - c)

    arguments = [
        pltpu.make_async_copy(src, dst, in_s.at[n])
        for n, (src, dst) in enumerate(((hid_hbm, hid), (emb_hbm, emb), (tgt_hbm, tgt), (pri_hbm, pri)))
    ]
    for argument in arguments:
        argument.start()

    partners = [sibling]
    partners += [device(x, (y + d) % NY, z, c) for d in (1, 2, 6, 7)]
    partners += [device(x, y, (z + d) % NZ, c) for d in (1, 2, 4, 6, 7)]
    partners += [x_dev(d) for d in (1, 2, 3)]
    barrier = pltpu.get_barrier_semaphore()
    for partner in partners:
        pl.semaphore_signal(barrier, inc=1, device_id=partner, device_id_type=MESH)

    for argument in arguments:
        argument.wait()
    for lo in range(0, QUARTER, 128):
        hi = min(lo + 128, QUARTER)
        hidn[:, lo:hi] = hid[lo:hi, :].astype(F32).T.astype(BF16)
    t = tgt[...]
    b = t // 8
    t_dp, t_k = b // 4, b % 4
    t_z = 2 * t_k + t_dp // (2 * NY * NX)
    place = (t_dp // (2 * NY) % NX) * ROWS + (t_z * NY + t_dp // 2 % NY) * PIECE + t_dp % 2 * 8 + t % 8
    meta[x] = jnp.concatenate([place.astype(F32), pri[...], jnp.zeros((6, TOK), F32)], axis=0)
    pl.semaphore_wait(barrier, len(partners))

    def received(ref, recv):
        copy(ref, ref, e_s.at[0], recv, sibling).wait_recv()

    def sent(ref, send):
        copy(ref, ref, send, e_s.at[1], sibling).wait_send()

    def copy(src, dst, send, recv, where):
        return pltpu.make_async_remote_copy(
            src_ref=src, dst_ref=dst, send_sem=send, recv_sem=recv,
            device_id=where, device_id_type=MESH,
        )

    e_copy = copy(emb, ebuf, e_s.at[0], e_s.at[1], sibling)
    e_copy.start()

    def set_rows(kk):
        return pl.ds(pl.multiple_of(kk * SET, SET), SET)

    def hidden_set(d):
        kk = (k + d) % NK
        return copy(hidn.at[set_rows(kk)], hb.at[x, k], ha_s.at[0], ha_r.at[d - 1], k_dev(kk))

    def hidden_x(j, d):
        ref = hb.at[x, j]
        return copy(ref, ref, hx_s.at[0], hx_r.at[0], x_dev(d))

    def hidden_on(d):
        received(hb.at[x, (k + NK - d) % NK], ha_r.at[d - 1])
        for e in (1, 3, 2):
            hidden_x((k + NK - d) % NK, e).start()

    def to_x(buf, send, recv, d):
        return copy(buf.at[x], buf.at[x], send.at[0], recv.at[0], x_dev(d))

    hb[x, k] = hidn[set_rows(k), :]
    e_copy.wait()
    mine, other = emb[...], ebuf[...]
    rows = jnp.concatenate(
        [jnp.where(c == 0, mine, other), jnp.where(c == 0, other, mine)], axis=0
    )
    g[at_row(z * NY + y), :] = rearranged(
        [rows[:, j * QUARTER:(j + 1) * QUARTER] for j in range(NK)]
    )

    def bring_in(h):
        outer, inner = (z, y) if h == 0 else (y, z)
        spans = (slice(0, SPLIT), slice(SPLIT, D))

        def number(o, i):
            return o * 8 + i if h == 0 else i * 8 + o

        def ring_dev(o, i):
            return device(x, i, o, c) if h == 0 else device(x, o, i, c)

        outer_next = ring_dev((outer + 1) % 8, inner)
        outer_last = ring_dev((outer + 7) % 8, inner)

        def piece(n, share):
            return g.at[at_row(n), spans[share]]

        def to_ring(o, i, where, recv):
            ref = piece(number(o, i), h)
            copy(ref, ref, g_s.at[0], g_r.at[recv], where).start()

        def to_inner(i, d, recv):
            to_ring(outer, i, ring_dev(outer, (inner + d + 8) % 8), recv)

        def to_sibling(o, i):
            ref = piece(number(o, i), h)
            copy(ref, ref, s_s.at[0], s_r.at[o], sibling).start()

        def to_outer(m):
            i = (inner + ring_offset(m) + 8) % 8
            to_ring(outer, i, outer_next, 8 + m)
            to_ring(outer, i, outer_last, 8 + m)

        for m, d in ((1, 1), (2, -1), (3, 2), (4, -2)):
            to_inner(inner, d, m)
        for e in (1, 3, 2):
            hidden_x(k, e).start()
        for d in (1, 2, 3):
            to_x(meta, m_s, m_r, d).start()

        def first(start, end, outward):
            for m in range(start, end):
                i = (inner + ring_offset(m) + 8) % 8
                received(piece(number(outer, i), h), g_r.at[m])
                for to, d in {3: ((5, 1), (7, 2)), 4: ((6, -1),)}.get(m, ()):
                    to_inner(i, d, to)
                if outward:
                    to_outer(m)
                to_sibling(outer, i)

        def second(ring, start, end):
            up, down = (outer + 8 - ring) % 8, (outer + ring) % 8

            def step(m, carry):
                i = (inner + ring_offset(m) + 8) % 8
                received(g.at[0:2 * PIECE, spans[h]], g_r.at[ring * 8 + m])
                to = (ring + 1) * 8 + m
                if ring == 3:
                    pl.when(m % 2 == 1)(lambda: to_ring(up, i, outer_next, to))
                    pl.when(m % 2 == 0)(lambda: to_ring(down, i, outer_last, to))
                else:
                    to_ring(up, i, outer_next, to)
                    to_ring(down, i, outer_last, to)
                to_sibling(up, i)
                to_sibling(down, i)
                return carry

            lax.fori_loop(start, end, step, 0)

        def logits(share, offsets):
            o0 = outer if share == h else inner
            by_z = share == 0
            starts = []
            for r in offsets:
                o = (o0 + r) % 8
                if by_z:
                    starts.append((pl.multiple_of(o * BLOCK, BLOCK), BLOCK))
                else:
                    starts += [(pl.multiple_of((i * 8 + o) * PIECE, PIECE), PIECE) for i in range(8)]
            left = jnp.concatenate([g[pl.ds(a, n), spans[share]] for a, n in starts], axis=0)
            value = lax.dot_general(
                left, ht[:, spans[share]], (((1,), (1,)), ((), ())), preferred_element_type=F32
            )
            at = 0
            for a, n in starts:
                lt[share, pl.ds(a, n), :] = value[at:at + n]
                at += n

        def await_sibling(r):
            rows = BLOCK - PIECE if isinstance(r, int) and r == 0 else BLOCK
            received(g.at[0:rows, spans[1 - h]], s_r.at[(inner + r) % 8])

        def features():
            received(hb.at[0:NX - 1], hx_r.at[0])
            for xx in range(NX):
                ht[xx * SET:(xx + 1) * SET, :] = rearranged([hb[xx, j] for j in range(NK)])

        def own_logits(r):
            logits(h, (r,) if r % 4 == 0 else (r, 8 - r))

        def sibling_logits(r):
            for b in (r,) if r % 4 == 0 else (r, 8 - r):
                await_sibling(b)
            logits(1 - h, (r,) if r % 4 == 0 else (r, 8 - r))

        def opposite():
            across = (outer + 4) % 8
            for m in range(8):
                i = (inner + ring_offset(m) + 8) % 8
                received(piece(number(across, i), h), g_r.at[32 + m])
                to_sibling(across, i)

        acts = {
            "first": first, "outer": to_outer, "second": second, "opposite": opposite,
            "send": lambda d: hidden_set(d).start(), "pass": hidden_on, "features": features,
            "own": own_logits, "sibling": sibling_logits,
        }
        for act, *numbers in STEPS[h]:
            acts[act](*numbers)

        sent(g.at[0:ROWS - PIECE, spans[h]], g_s.at[0])
        sent(g.at[0:ROWS - PIECE, spans[h]], s_s.at[0])

    for core in (0, 1):
        pl.when(c == core)(functools.partial(bring_in, core))

    lane_set = lax.broadcasted_iota(jnp.int32, (8, TOK), 1) // SET
    received(meta.at[0:NX - 1], m_r.at[0])
    info = jnp.zeros((8, TOK), F32)
    for xx in range(NX):
        turned = pltpu.roll(meta[xx], (xx + NX - k) % NX * SET, axis=1)
        info = jnp.where(lane_set == xx, turned, info)
    column = info[0:1] - (x * ROWS).astype(F32)
    owned = (column >= 0.0) & (column < float(ROWS))
    prior = info[1:2]

    peaks = jnp.full((8, TOK), -jnp.inf, F32)
    for n in range(8):
        span = slice(n * BLOCK, (n + 1) * BLOCK)
        value = lt[0, span, :] + lt[1, span, :]
        lt[0, span, :] = value
        peaks = jnp.maximum(peaks, jnp.max(value.reshape(BLOCK // 8, 8, TOK), axis=0))
    peak = jnp.max(peaks, axis=0, keepdims=True)
    total = jnp.zeros((8, TOK), F32)
    target = jnp.zeros((8, TOK), F32)
    row_id = lax.broadcasted_iota(jnp.int32, (BLOCK, TOK), 0).astype(F32)
    for n in range(8):
        span = slice(n * BLOCK, (n + 1) * BLOCK)
        value = lt[0, span, :]
        hit = row_id == column - float(n * BLOCK)
        power = jnp.exp(value - peak)
        lt[1, span, :] = jnp.where(hit, 0.0, power)
        total += jnp.sum(power.reshape(BLOCK // 8, 8, TOK), axis=0)
        target += jnp.sum(jnp.where(hit, value, 0.0).reshape(BLOCK // 8, 8, TOK), axis=0)
    my_target = jnp.sum(target, axis=0, keepdims=True)
    stat[x] = jnp.concatenate(
        [peak, jnp.sum(total, axis=0, keepdims=True), my_target, jnp.zeros((5, TOK), F32)], axis=0
    )
    for d in (1, 2, 3):
        to_x(stat, t_s, t_r, d).start()

    column_t = jnp.broadcast_to(column, (8, TOK)).T[:, 0:1]
    lane_id = lax.broadcasted_iota(jnp.int32, (TOK, BLOCK), 1).astype(F32)
    for n in range(8):
        span = slice(n * BLOCK, (n + 1) * BLOCK)
        gl[0:TOK, span] = lt[1, span, :].T.astype(BF16)
        gl[TOK:, span] = jnp.where(lane_id == column_t - float(n * BLOCK), 1.0, 0.0).astype(BF16)

    units = ((2, 1), (2, 0), (1, 0), (3, 0), (1, 1), (3, 1), (0, 0), (0, 1))
    turns = (2, 1, 3, 0)
    parts, r1s, s2s, rds = (part_a, part_b), (r1_a, r1_b), (s2_a, s2_b), (rd_a, rd_b)
    r3s, zss, zrs = (r3_a, r3_b), (zs_a, zs_b), (zr_a, zr_b)

    def place_of(u):
        turn, p = units[u]
        return turns.index(turn), p

    def products(u, use):
        turn, p = units[u]
        j = (k + turn) % NK
        for lo, hi in ((0, 512), (512, PART_A)) if p == 0 else ((PART_A, MAIN),):
            at = pl.ds(pl.multiple_of(j * MAIN + lo, 128), hi - lo)
            use(lo - p * PART_A, jnp.dot(gl[...], g[:, at], preferred_element_type=F32))
        if p == 1:
            at = pl.ds(pl.multiple_of(NK * MAIN + j // 2 * 128, 128), 128)
            value = jnp.dot(gl[...], g[:, at], preferred_element_type=F32)
            use(MAIN - PART_A, pltpu.roll(value, j % 2 * REST, axis=1)[:, :REST])

    def weigh(u):
        q, p = place_of(u)

        def use(lo, value):
            for at in range(0, value.shape[1], 128):
                w = min(128, value.shape[1] - at)
                mixed = (
                    value[:TOK, at:at + w] * coef[0, :, :w] + value[TOK:, at:at + w] * coef[1, :, :w]
                )
                parts[p][q, :, lo + at:lo + at + w] = mixed.astype(BF16)

        return use

    def keep(u):
        def use(lo, value):
            raw[u, :, lo:lo + value.shape[1]] = value

        return use

    for u in range(KEPT):
        products(u, keep(u))

    received(stat.at[0:NX - 1], t_r.at[0])
    top = prior
    for xx in range(NX):
        top = jnp.maximum(top, stat[xx, 0:1, :])
    whole = jnp.exp(prior - top)
    logit = jnp.zeros((1, TOK), F32)
    for xx in range(NX):
        whole += stat[xx, 1:2, :] * jnp.exp(stat[xx, 0:1, :] - top)
        logit += stat[xx, 2:3, :]
    lse = top + jnp.log(whole)
    weights = jnp.concatenate(
        [jnp.exp(peak - lse), jnp.where(owned, jnp.exp(my_target - lse) - 1.0, 0.0),
         jnp.zeros((6, TOK), F32)], axis=0,
    ).T
    coef[0] = jnp.broadcast_to(weights[:, 0:1], (TOK, 128))
    coef[1] = jnp.broadcast_to(weights[:, 1:2], (TOK, 128))

    def x_rows(d):
        return pl.ds(pl.multiple_of((x + d) % NX * SET, SET), SET)

    def x_half(d, way):
        return pl.ds(pl.multiple_of((x + d) % NX * SET + way * SUB, SUB), SUB)

    ways = ((0, 1, 3), (1, 3, 1))

    def opposite_copy(u, way, d):
        q, p = place_of(u)
        return copy(parts[p].at[q, x_half(2, way)], r1s[p].at[q, way], o_s.at[p], o_r.at[u], x_dev(d))

    def direct_copy(u, way, d):
        q, p = place_of(u)
        return copy(parts[p].at[q, x_half(d, way)], rds[p].at[q, way], d_s.at[p], d_r.at[u], x_dev(d))

    def sum_copy(u, way, d):
        q, p = place_of(u)
        return copy(s2s[p].at[q, way], rds[p].at[q, 2 + way], q_s.at[p], d_r.at[u], x_dev(d))

    def straight_copy(p, d):
        return copy(parts[p].at[3, x_rows(d)], r3s[p].at[d - 1], w_s.at[p], w_r.at[p], x_dev(d))

    def z_copy(u):
        q, p = place_of(u)
        return copy(zss[p].at[q], zrs[p].at[q], z_s.at[p], z_r.at[u], k_dev((k + units[u][0]) % NK))

    def send_first(u):
        q, p = place_of(u)
        if q == 3:
            for d in (2, 1, 3):
                straight_copy(p, d).start()
            return
        for way, near, _ in ways:
            opposite_copy(u, way, near).start()
        for way, _, far in ways:
            direct_copy(u, way, far).start()

    def multiply(u):
        _, p = place_of(u)
        for lo in range(0, WIDTHS[p], 128):
            weigh(u)(lo, raw[u, :, lo:min(lo + 128, WIDTHS[p])])
        send_first(u)

    def add_first(u):
        q, p = place_of(u)
        received(r1s[p].at[q], o_r.at[u])
        for way, near, _ in ways:
            s2s[p][q, way] = (
                parts[p][q, x_half(near, way), :].astype(F32) + r1s[p][q, way].astype(F32)
            ).astype(BF16)
            sum_copy(u, way, near).start()

    def add_last(u):
        q, p = place_of(u)
        received(rds[p].at[q], d_r.at[u])
        for way in (0, 1):
            zss[p][q, way * SUB:(way + 1) * SUB, :] = (
                parts[p][q, x_half(0, way), :].astype(F32)
                + rds[p][q, way].astype(F32) + rds[p][q, 2 + way].astype(F32)
            ).astype(BF16)
        z_copy(u).start()

    def own(p):
        received(r3s[p], w_r.at[p])
        value = parts[p][3, x_rows(0), :].astype(F32)
        for d in (1, 2, 3):
            value += r3s[p][d - 1].astype(F32)
        out[set_rows(k), p * PART_A:p * PART_A + WIDTHS[p]] = value.astype(BF16)

    def finish(u):
        q, p = place_of(u)
        received(zrs[p].at[q], z_r.at[u])
        rows = set_rows((k + NK - units[u][0]) % NK)
        out[rows, p * PART_A:p * PART_A + WIDTHS[p]] = zrs[p][q]

    multiply(0)
    lbuf[k] = jnp.broadcast_to(lse - logit, (8, TOK))

    def loss_to(d):
        return copy(lbuf.at[k], lbuf.at[k], l_s.at[0], l_r.at[0], k_dev((k + d) % NK))

    for d in (1, 2, 3):
        loss_to(d).start()
    multiply(1)
    multiply(2)
    for u in range(KEPT, 8):
        products(u, keep(u))
    add_first(0)
    multiply(3)
    add_first(1)
    multiply(4)
    add_first(2)
    multiply(5)
    add_first(3)
    add_last(0)
    add_first(4)
    add_last(1)
    add_first(5)
    add_last(2)
    add_last(3)
    multiply(6)
    add_last(4)
    multiply(7)
    add_last(5)

    received(lbuf.at[0:NK - 1], l_r.at[0])
    result = jnp.zeros((8, TOK), F32)
    for kk in range(NK):
        turned = pltpu.roll(lbuf[kk], (kk + NX - x) % NX * SET, axis=1)
        result = jnp.where(lane_set == kk, turned, result)
    loss[...] = result[0:1]

    finish(0)
    finish(1)
    own(0)
    own(1)
    for u in (2, 4, 3, 5):
        finish(u)

    sent(hidn.at[0:TOK - SET], ha_s.at[0])
    sent(hb.at[0:NX - 1], hx_s.at[0])
    for buf, send in ((meta, m_s), (stat, t_s), (lbuf, l_s)):
        sent(buf.at[0:3], send.at[0])
    for p in (0, 1):
        sent(r1s[p], o_s.at[p])
        sent(r1s[p], d_s.at[p])
        sent(r1s[p], q_s.at[p])
        sent(r3s[p], w_s.at[p])
        sent(zss[p], z_s.at[p])


def body(hidden_states, embedding, targets, prior_lse):
    dma = pltpu.SemaphoreType.DMA
    hbm = pl.BlockSpec(memory_space=pltpu.HBM)
    vmem = pl.BlockSpec(memory_space=pltpu.VMEM)
    arguments = (hidden_states.T, embedding, targets.reshape(1, TOK), prior_lse.reshape(1, TOK))
    pair = [(WIDTHS[0],), (WIDTHS[1],)]
    loss, grad = pl.pallas_call(
        kernel,
        out_shape=(
            jax.ShapeDtypeStruct((1, TOK), F32),
            jax.ShapeDtypeStruct((TOK, QUARTER), BF16),
        ),
        in_specs=[hbm] * 4,
        out_specs=(vmem, vmem),
        scratch_shapes=[
            pltpu.VMEM((QUARTER, TOK), BF16),
            pltpu.VMEM((8, D), BF16),
            pltpu.VMEM((1, TOK), jnp.int32),
            pltpu.VMEM((1, TOK), F32),
            pltpu.VMEM((ROWS, D), BF16),
            pltpu.VMEM((8, D), BF16),
            pltpu.VMEM((TOK, QUARTER), BF16),
            pltpu.VMEM((NX, NK, SET, QUARTER), BF16),
            pltpu.VMEM((TOK, D), BF16),
            pltpu.VMEM((2, ROWS, TOK), F32),
            pltpu.VMEM((2 * TOK, ROWS), BF16),
            pltpu.VMEM((8, 2 * TOK, WIDTHS[0]), F32),
            pltpu.VMEM((2, TOK, 128), F32),
            pltpu.VMEM((NX, 8, TOK), F32),
            pltpu.VMEM((NX, 8, TOK), F32),
            pltpu.VMEM((NK, 8, TOK), F32),
            *[pltpu.VMEM((NK, TOK) + w, BF16) for w in pair],
            *[pltpu.VMEM((NK - 1, 2, SUB) + w, BF16) for w in pair * 2],
            *[pltpu.VMEM((NK - 1, 4, SUB) + w, BF16) for w in pair],
            *[pltpu.VMEM((NX - 1, SET) + w, BF16) for w in pair],
            *[pltpu.VMEM((NK - 1, SET) + w, BF16) for w in pair * 2],
            *[dma((n,)) for n in (4, 2, 40, 8, 1, 1, 1, 3, 1, 1)],
            *[dma((n,)) for n in (1, 1, 1, 1, 1, 1, 2, 6, 2, 6, 2, 2, 2, 2, 6)],
        ],
        compiler_params=pltpu.CompilerParams(
            collective_id=0, has_side_effects=True, vmem_limit_bytes=48 << 20
        ),
        cost_estimate=pl.CostEstimate(
            flops=6 * TOK * ROWS * D, bytes_accessed=4 * TOK * D, transcendentals=TOK * ROWS
        ),
    )(*[pltpu.with_memory_space_constraint(a, pltpu.HBM) for a in arguments])
    return loss.reshape(TOK), grad


def solution(mesh):
    placed = (P("dp", "tensor"), P(("dp", "tensor"), None), P("dp"), P("dp"))
    return jax.shard_map(
        body, mesh=mesh, in_specs=placed, out_specs=(P("dp"), P("dp", "tensor")), check_vma=False
    )
```

```python
import functools

import jax
import jax.numpy as jnp
from jax import lax
from jax.experimental import pallas as pl
from jax.experimental.pallas import tpu as pltpu
from jax.sharding import PartitionSpec as P

MESH = pl.DeviceIdType.MESH
BF16 = jnp.bfloat16
F32 = jnp.float32
NX, NY, NZ, NK = 4, 8, 8, 4
D = 5376
QUARTER = D // NK
MAIN = QUARTER // 128 * 128
REST = QUARTER - MAIN
PART_A = 768
WIDTHS = (PART_A, QUARTER - PART_A)
KEPT = 5
SPLIT = 18 * 128
TOK = 128
SET = TOK // NK
SUB = SET // 2
PIECE = 16
BLOCK = 8 * PIECE
ROWS = NY * NZ * PIECE


STEPS = (
    (
        ("first", 1, 3, False), ("send", 1), ("send", 3), ("send", 2), ("outer", 0), ("outer", 1),
        ("first", 3, 8, False), ("outer", 2), ("outer", 3), ("outer", 4), ("pass", 1), ("pass", 3),
        ("pass", 2), ("outer", 5), ("outer", 6), ("outer", 7), ("second", 1, 0, 8),
        ("second", 2, 0, 5), ("features",), ("own", 0), ("sibling", 0), ("second", 2, 5, 8),
        ("own", 1), ("second", 3, 0, 4), ("sibling", 1), ("own", 2), ("second", 3, 4, 8),
        ("sibling", 2), ("own", 3), ("sibling", 3), ("opposite",), ("own", 4), ("sibling", 4),
    ),
    (
        ("outer", 0), ("first", 1, 3, True), ("send", 1), ("send", 3), ("send", 2),
        ("second", 1, 0, 1), ("first", 3, 5, True), ("second", 2, 0, 1), ("pass", 1), ("pass", 3),
        ("pass", 2), ("second", 1, 1, 5), ("first", 5, 8, True), ("second", 2, 1, 5),
        ("second", 1, 5, 8), ("features",), ("own", 0), ("sibling", 0), ("own", 1),
        ("second", 2, 5, 8), ("second", 3, 0, 4), ("sibling", 1), ("own", 2), ("second", 3, 4, 8),
        ("sibling", 2), ("own", 3), ("sibling", 3), ("opposite",), ("own", 4), ("sibling", 4),
    ),
)


def device(x, y, z, c):
    return (((z % 2) * NX + x) * NY + y) * 2 + c, z // 2


def at_row(row):
    return pl.ds(pl.multiple_of(row * PIECE, PIECE), PIECE)


def ring_offset(m):
    return ((m + 1) // 2) * (1 - 2 * (m % 2))


def rearranged(quarters):
    return jnp.concatenate(
        [q[:, :MAIN] for q in quarters] + [q[:, MAIN:] for q in quarters], axis=1
    )


def kernel(
    hid_hbm, emb_hbm, tgt_hbm, pri_hbm, loss, out,
    hid, emb, tgt, pri, g, ebuf, hidn, hb, ht, lt, gl, raw, coef, meta, stat, lbuf,
    part_a, part_b, r1_a, r1_b, s2_a, s2_b, rd_a, rd_b, r3_a, r3_b, zs_a, zs_b, zr_a, zr_b,
    in_s, e_s, g_r, s_r, g_s, s_s, ha_s, ha_r, hx_s, hx_r,
    m_s, m_r, t_s, t_r, l_s, l_r, o_s, o_r, d_s, d_r, q_s, w_s, w_r, z_s, z_r,
):
    dp = lax.axis_index("dp")
    k = lax.axis_index("tensor")
    c = dp % 2
    y = dp // 2 % NY
    x = dp // (2 * NY) % NX
    zl = dp // (2 * NY * NX)
    z = 2 * k + zl

    def x_dev(d):
        return device((x + d) % NX, y, z, c)

    def k_dev(kk):
        return device(x, y, 2 * kk + zl, c)

    sibling = device(x, y, z, 1 - c)

    arguments = [
        pltpu.make_async_copy(src, dst, in_s.at[n])
        for n, (src, dst) in enumerate(((hid_hbm, hid), (emb_hbm, emb), (tgt_hbm, tgt), (pri_hbm, pri)))
    ]
    for argument in arguments:
        argument.start()

    partners = [sibling]
    partners += [device(x, (y + d) % NY, z, c) for d in (1, 2, 6, 7)]
    partners += [device(x, y, (z + d) % NZ, c) for d in (1, 2, 4, 6, 7)]
    partners += [x_dev(d) for d in (1, 2, 3)]
    barrier = pltpu.get_barrier_semaphore()
    for partner in partners:
        pl.semaphore_signal(barrier, inc=1, device_id=partner, device_id_type=MESH)

    for argument in arguments:
        argument.wait()
    for lo in range(0, QUARTER, 128):
        hi = min(lo + 128, QUARTER)
        hidn[:, lo:hi] = hid[lo:hi, :].astype(F32).T.astype(BF16)
    t = tgt[...]
    b = t // 8
    t_dp, t_k = b // 4, b % 4
    t_z = 2 * t_k + t_dp // (2 * NY * NX)
    place = (t_dp // (2 * NY) % NX) * ROWS + (t_z * NY + t_dp // 2 % NY) * PIECE + t_dp % 2 * 8 + t % 8
    meta[x] = jnp.concatenate([place.astype(F32), pri[...], jnp.zeros((6, TOK), F32)], axis=0)
    pl.semaphore_wait(barrier, len(partners))

    def received(ref, recv):
        copy(ref, ref, e_s.at[0], recv, sibling).wait_recv()

    def sent(ref, send):
        copy(ref, ref, send, e_s.at[1], sibling).wait_send()

    def copy(src, dst, send, recv, where):
        return pltpu.make_async_remote_copy(
            src_ref=src, dst_ref=dst, send_sem=send, recv_sem=recv,
            device_id=where, device_id_type=MESH,
        )

    e_copy = copy(emb, ebuf, e_s.at[0], e_s.at[1], sibling)
    e_copy.start()

    def set_rows(kk):
        return pl.ds(pl.multiple_of(kk * SET, SET), SET)

    def hidden_set(d):
        kk = (k + d) % NK
        return copy(hidn.at[set_rows(kk)], hb.at[x, k], ha_s.at[0], ha_r.at[d - 1], k_dev(kk))

    def hidden_x(j, d):
        ref = hb.at[x, j]
        return copy(ref, ref, hx_s.at[0], hx_r.at[0], x_dev(d))

    def hidden_on(d):
        received(hb.at[x, (k + NK - d) % NK], ha_r.at[d - 1])
        for e in (1, 3, 2):
            hidden_x((k + NK - d) % NK, e).start()

    def to_x(buf, send, recv, d):
        return copy(buf.at[x], buf.at[x], send.at[0], recv.at[0], x_dev(d))

    hb[x, k] = hidn[set_rows(k), :]
    e_copy.wait()
    mine, other = emb[...], ebuf[...]
    rows = jnp.concatenate(
        [jnp.where(c == 0, mine, other), jnp.where(c == 0, other, mine)], axis=0
    )
    g[at_row(z * NY + y), :] = rearranged(
        [rows[:, j * QUARTER:(j + 1) * QUARTER] for j in range(NK)]
    )

    def bring_in(h):
        outer, inner = (z, y) if h == 0 else (y, z)
        spans = (slice(0, SPLIT), slice(SPLIT, D))

        def number(o, i):
            return o * 8 + i if h == 0 else i * 8 + o

        def ring_dev(o, i):
            return device(x, i, o, c) if h == 0 else device(x, o, i, c)

        outer_next = ring_dev((outer + 1) % 8, inner)
        outer_last = ring_dev((outer + 7) % 8, inner)

        def piece(n, share):
            return g.at[at_row(n), spans[share]]

        def to_ring(o, i, where, recv):
            ref = piece(number(o, i), h)
            copy(ref, ref, g_s.at[0], g_r.at[recv], where).start()

        def to_inner(i, d, recv):
            to_ring(outer, i, ring_dev(outer, (inner + d + 8) % 8), recv)

        def to_sibling(o, i):
            ref = piece(number(o, i), h)
            copy(ref, ref, s_s.at[0], s_r.at[o], sibling).start()

        def to_outer(m):
            i = (inner + ring_offset(m) + 8) % 8
            to_ring(outer, i, outer_next, 8 + m)
            to_ring(outer, i, outer_last, 8 + m)

        for m, d in ((1, 1), (2, -1), (3, 2), (4, -2)):
            to_inner(inner, d, m)
        for e in (1, 3, 2):
            hidden_x(k, e).start()
        for d in (1, 2, 3):
            to_x(meta, m_s, m_r, d).start()

        def first(start, end, outward):
            for m in range(start, end):
                i = (inner + ring_offset(m) + 8) % 8
                received(piece(number(outer, i), h), g_r.at[m])
                for to, d in {3: ((5, 1), (7, 2)), 4: ((6, -1),)}.get(m, ()):
                    to_inner(i, d, to)
                if outward:
                    to_outer(m)
                to_sibling(outer, i)

        def second(ring, start, end):
            up, down = (outer + 8 - ring) % 8, (outer + ring) % 8

            def step(m, carry):
                i = (inner + ring_offset(m) + 8) % 8
                received(g.at[0:2 * PIECE, spans[h]], g_r.at[ring * 8 + m])
                to = (ring + 1) * 8 + m
                if ring == 3:
                    pl.when(m % 2 == 1)(lambda: to_ring(up, i, outer_next, to))
                    pl.when(m % 2 == 0)(lambda: to_ring(down, i, outer_last, to))
                else:
                    to_ring(up, i, outer_next, to)
                    to_ring(down, i, outer_last, to)
                to_sibling(up, i)
                to_sibling(down, i)
                return carry

            lax.fori_loop(start, end, step, 0)

        def logits(share, offsets):
            o0 = outer if share == h else inner
            by_z = share == 0
            starts = []
            for r in offsets:
                o = (o0 + r) % 8
                if by_z:
                    starts.append((pl.multiple_of(o * BLOCK, BLOCK), BLOCK))
                else:
                    starts += [(pl.multiple_of((i * 8 + o) * PIECE, PIECE), PIECE) for i in range(8)]
            left = jnp.concatenate([g[pl.ds(a, n), spans[share]] for a, n in starts], axis=0)
            value = lax.dot_general(
                left, ht[:, spans[share]], (((1,), (1,)), ((), ())), preferred_element_type=F32
            )
            at = 0
            for a, n in starts:
                lt[share, pl.ds(a, n), :] = value[at:at + n]
                at += n

        def await_sibling(r):
            rows = BLOCK - PIECE if isinstance(r, int) and r == 0 else BLOCK
            received(g.at[0:rows, spans[1 - h]], s_r.at[(inner + r) % 8])

        def features():
            received(hb.at[0:NX - 1], hx_r.at[0])
            for xx in range(NX):
                ht[xx * SET:(xx + 1) * SET, :] = rearranged([hb[xx, j] for j in range(NK)])

        def own_logits(r):
            logits(h, (r,) if r % 4 == 0 else (r, 8 - r))

        def sibling_logits(r):
            for b in (r,) if r % 4 == 0 else (r, 8 - r):
                await_sibling(b)
            logits(1 - h, (r,) if r % 4 == 0 else (r, 8 - r))

        def opposite():
            across = (outer + 4) % 8
            for m in range(8):
                i = (inner + ring_offset(m) + 8) % 8
                received(piece(number(across, i), h), g_r.at[32 + m])
                to_sibling(across, i)

        acts = {
            "first": first, "outer": to_outer, "second": second, "opposite": opposite,
            "send": lambda d: hidden_set(d).start(), "pass": hidden_on, "features": features,
            "own": own_logits, "sibling": sibling_logits,
        }
        for act, *numbers in STEPS[h]:
            acts[act](*numbers)

        sent(g.at[0:ROWS - PIECE, spans[h]], g_s.at[0])
        sent(g.at[0:ROWS - PIECE, spans[h]], s_s.at[0])

    for core in (0, 1):
        pl.when(c == core)(functools.partial(bring_in, core))

    lane_set = lax.broadcasted_iota(jnp.int32, (8, TOK), 1) // SET
    received(meta.at[0:NX - 1], m_r.at[0])
    info = jnp.zeros((8, TOK), F32)
    for xx in range(NX):
        turned = pltpu.roll(meta[xx], (xx + NX - k) % NX * SET, axis=1)
        info = jnp.where(lane_set == xx, turned, info)
    column = info[0:1] - (x * ROWS).astype(F32)
    owned = (column >= 0.0) & (column < float(ROWS))
    prior = info[1:2]

    peaks = jnp.full((8, TOK), -jnp.inf, F32)
    for n in range(8):
        span = slice(n * BLOCK, (n + 1) * BLOCK)
        value = lt[0, span, :] + lt[1, span, :]
        lt[0, span, :] = value
        peaks = jnp.maximum(peaks, jnp.max(value.reshape(BLOCK // 8, 8, TOK), axis=0))
    peak = jnp.max(peaks, axis=0, keepdims=True)
    total = jnp.zeros((8, TOK), F32)
    target = jnp.zeros((8, TOK), F32)
    row_id = lax.broadcasted_iota(jnp.int32, (BLOCK, TOK), 0).astype(F32)
    for n in range(8):
        span = slice(n * BLOCK, (n + 1) * BLOCK)
        value = lt[0, span, :]
        hit = row_id == column - float(n * BLOCK)
        power = jnp.exp(value - peak)
        lt[1, span, :] = jnp.where(hit, 0.0, power)
        total += jnp.sum(power.reshape(BLOCK // 8, 8, TOK), axis=0)
        target += jnp.sum(jnp.where(hit, value, 0.0).reshape(BLOCK // 8, 8, TOK), axis=0)
    my_target = jnp.sum(target, axis=0, keepdims=True)
    stat[x] = jnp.concatenate(
        [peak, jnp.sum(total, axis=0, keepdims=True), my_target, jnp.zeros((5, TOK), F32)], axis=0
    )
    for d in (1, 2, 3):
        to_x(stat, t_s, t_r, d).start()

    column_t = jnp.broadcast_to(column, (8, TOK)).T[:, 0:1]
    lane_id = lax.broadcasted_iota(jnp.int32, (TOK, BLOCK), 1).astype(F32)
    for n in range(8):
        span = slice(n * BLOCK, (n + 1) * BLOCK)
        gl[0:TOK, span] = lt[1, span, :].T.astype(BF16)
        gl[TOK:, span] = jnp.where(lane_id == column_t - float(n * BLOCK), 1.0, 0.0).astype(BF16)

    units = ((2, 1), (2, 0), (1, 0), (3, 0), (1, 1), (3, 1), (0, 0), (0, 1))
    turns = (2, 1, 3, 0)
    parts, r1s, s2s, rds = (part_a, part_b), (r1_a, r1_b), (s2_a, s2_b), (rd_a, rd_b)
    r3s, zss, zrs = (r3_a, r3_b), (zs_a, zs_b), (zr_a, zr_b)

    def place_of(u):
        turn, p = units[u]
        return turns.index(turn), p

    def products(u, use):
        turn, p = units[u]
        j = (k + turn) % NK
        for lo, hi in ((0, 512), (512, PART_A)) if p == 0 else ((PART_A, MAIN),):
            at = pl.ds(pl.multiple_of(j * MAIN + lo, 128), hi - lo)
            use(lo - p * PART_A, jnp.dot(gl[...], g[:, at], preferred_element_type=F32))
        if p == 1:
            at = pl.ds(pl.multiple_of(NK * MAIN + j // 2 * 128, 128), 128)
            value = jnp.dot(gl[...], g[:, at], preferred_element_type=F32)
            use(MAIN - PART_A, pltpu.roll(value, j % 2 * REST, axis=1)[:, :REST])

    def weigh(u):
        q, p = place_of(u)

        def use(lo, value):
            for at in range(0, value.shape[1], 128):
                w = min(128, value.shape[1] - at)
                mixed = (
                    value[:TOK, at:at + w] * coef[0, :, :w] + value[TOK:, at:at + w] * coef[1, :, :w]
                )
                parts[p][q, :, lo + at:lo + at + w] = mixed.astype(BF16)

        return use

    def keep(u):
        def use(lo, value):
            raw[u, :, lo:lo + value.shape[1]] = value

        return use

    for u in range(KEPT):
        products(u, keep(u))

    received(stat.at[0:NX - 1], t_r.at[0])
    top = prior
    for xx in range(NX):
        top = jnp.maximum(top, stat[xx, 0:1, :])
    whole = jnp.exp(prior - top)
    logit = jnp.zeros((1, TOK), F32)
    for xx in range(NX):
        whole += stat[xx, 1:2, :] * jnp.exp(stat[xx, 0:1, :] - top)
        logit += stat[xx, 2:3, :]
    lse = top + jnp.log(whole)
    weights = jnp.concatenate(
        [jnp.exp(peak - lse), jnp.where(owned, jnp.exp(my_target - lse) - 1.0, 0.0),
         jnp.zeros((6, TOK), F32)], axis=0,
    ).T
    coef[0] = jnp.broadcast_to(weights[:, 0:1], (TOK, 128))
    coef[1] = jnp.broadcast_to(weights[:, 1:2], (TOK, 128))

    def x_rows(d):
        return pl.ds(pl.multiple_of((x + d) % NX * SET, SET), SET)

    def x_half(d, way):
        return pl.ds(pl.multiple_of((x + d) % NX * SET + way * SUB, SUB), SUB)

    ways = ((0, 1, 3), (1, 3, 1))

    def opposite_copy(u, way, d):
        q, p = place_of(u)
        return copy(parts[p].at[q, x_half(2, way)], r1s[p].at[q, way], o_s.at[p], o_r.at[u], x_dev(d))

    def direct_copy(u, way, d):
        q, p = place_of(u)
        return copy(parts[p].at[q, x_half(d, way)], rds[p].at[q, way], d_s.at[p], d_r.at[u], x_dev(d))

    def sum_copy(u, way, d):
        q, p = place_of(u)
        return copy(s2s[p].at[q, way], rds[p].at[q, 2 + way], q_s.at[p], d_r.at[u], x_dev(d))

    def straight_copy(p, d):
        return copy(parts[p].at[3, x_rows(d)], r3s[p].at[d - 1], w_s.at[p], w_r.at[p], x_dev(d))

    def z_copy(u):
        q, p = place_of(u)
        return copy(zss[p].at[q], zrs[p].at[q], z_s.at[p], z_r.at[u], k_dev((k + units[u][0]) % NK))

    def send_first(u):
        q, p = place_of(u)
        if q == 3:
            for d in (2, 1, 3):
                straight_copy(p, d).start()
            return
        for way, near, _ in ways:
            opposite_copy(u, way, near).start()
        for way, _, far in ways:
            direct_copy(u, way, far).start()

    def multiply(u):
        _, p = place_of(u)
        for lo in range(0, WIDTHS[p], 128):
            weigh(u)(lo, raw[u, :, lo:min(lo + 128, WIDTHS[p])])
        send_first(u)

    def add_first(u):
        q, p = place_of(u)
        received(r1s[p].at[q], o_r.at[u])
        for way, near, _ in ways:
            s2s[p][q, way] = (
                parts[p][q, x_half(near, way), :].astype(F32) + r1s[p][q, way].astype(F32)
            ).astype(BF16)
            sum_copy(u, way, near).start()

    def add_last(u):
        q, p = place_of(u)
        received(rds[p].at[q], d_r.at[u])
        for way in (0, 1):
            zss[p][q, way * SUB:(way + 1) * SUB, :] = (
                parts[p][q, x_half(0, way), :].astype(F32)
                + rds[p][q, way].astype(F32) + rds[p][q, 2 + way].astype(F32)
            ).astype(BF16)
        z_copy(u).start()

    def own(p):
        received(r3s[p], w_r.at[p])
        value = parts[p][3, x_rows(0), :].astype(F32)
        for d in (1, 2, 3):
            value += r3s[p][d - 1].astype(F32)
        out[set_rows(k), p * PART_A:p * PART_A + WIDTHS[p]] = value.astype(BF16)

    def finish(u):
        q, p = place_of(u)
        received(zrs[p].at[q], z_r.at[u])
        rows = set_rows((k + NK - units[u][0]) % NK)
        out[rows, p * PART_A:p * PART_A + WIDTHS[p]] = zrs[p][q]

    multiply(0)
    lbuf[k] = jnp.broadcast_to(lse - logit, (8, TOK))

    def loss_to(d):
        return copy(lbuf.at[k], lbuf.at[k], l_s.at[0], l_r.at[0], k_dev((k + d) % NK))

    for d in (1, 2, 3):
        loss_to(d).start()
    multiply(1)
    multiply(2)
    for u in range(KEPT, 8):
        products(u, keep(u))
    add_first(0)
    multiply(3)
    add_first(1)
    multiply(4)
    add_first(2)
    multiply(5)
    add_first(3)
    add_last(0)
    add_first(4)
    add_last(1)
    add_first(5)
    add_last(2)
    add_last(3)
    multiply(6)
    add_last(4)
    multiply(7)
    add_last(5)

    received(lbuf.at[0:NK - 1], l_r.at[0])
    result = jnp.zeros((8, TOK), F32)
    for kk in range(NK):
        turned = pltpu.roll(lbuf[kk], (kk + NX - x) % NX * SET, axis=1)
        result = jnp.where(lane_set == kk, turned, result)
    loss[...] = result[0:1]

    finish(0)
    finish(1)
    own(0)
    own(1)
    for u in (2, 4, 3, 5):
        finish(u)

    sent(hidn.at[0:TOK - SET], ha_s.at[0])
    sent(hb.at[0:NX - 1], hx_s.at[0])
    for buf, send in ((meta, m_s), (stat, t_s), (lbuf, l_s)):
        sent(buf.at[0:3], send.at[0])
    for p in (0, 1):
        sent(r1s[p], o_s.at[p])
        sent(r1s[p], d_s.at[p])
        sent(r1s[p], q_s.at[p])
        sent(r3s[p], w_s.at[p])
        sent(zss[p], z_s.at[p])


def body(hidden_states, embedding, targets, prior_lse):
    dma = pltpu.SemaphoreType.DMA
    hbm = pl.BlockSpec(memory_space=pltpu.HBM)
    vmem = pl.BlockSpec(memory_space=pltpu.VMEM)
    arguments = (hidden_states.T, embedding, targets.reshape(1, TOK), prior_lse.reshape(1, TOK))
    pair = [(WIDTHS[0],), (WIDTHS[1],)]
    loss, grad = pl.pallas_call(
        kernel,
        out_shape=(
            jax.ShapeDtypeStruct((1, TOK), F32),
            jax.ShapeDtypeStruct((TOK, QUARTER), BF16),
        ),
        in_specs=[hbm] * 4,
        out_specs=(vmem, vmem),
        scratch_shapes=[
            pltpu.VMEM((QUARTER, TOK), BF16),
            pltpu.VMEM((8, D), BF16),
            pltpu.VMEM((1, TOK), jnp.int32),
            pltpu.VMEM((1, TOK), F32),
            pltpu.VMEM((ROWS, D), BF16),
            pltpu.VMEM((8, D), BF16),
            pltpu.VMEM((TOK, QUARTER), BF16),
            pltpu.VMEM((NX, NK, SET, QUARTER), BF16),
            pltpu.VMEM((TOK, D), BF16),
            pltpu.VMEM((2, ROWS, TOK), F32),
            pltpu.VMEM((2 * TOK, ROWS), BF16),
            pltpu.VMEM((8, 2 * TOK, WIDTHS[0]), F32),
            pltpu.VMEM((2, TOK, 128), F32),
            pltpu.VMEM((NX, 8, TOK), F32),
            pltpu.VMEM((NX, 8, TOK), F32),
            pltpu.VMEM((NK, 8, TOK), F32),
            *[pltpu.VMEM((NK, TOK) + w, BF16) for w in pair],
            *[pltpu.VMEM((NK - 1, 2, SUB) + w, BF16) for w in pair * 2],
            *[pltpu.VMEM((NK - 1, 4, SUB) + w, BF16) for w in pair],
            *[pltpu.VMEM((NX - 1, SET) + w, BF16) for w in pair],
            *[pltpu.VMEM((NK - 1, SET) + w, BF16) for w in pair * 2],
            *[dma((n,)) for n in (4, 2, 40, 8, 1, 1, 1, 3, 1, 1)],
            *[dma((n,)) for n in (1, 1, 1, 1, 1, 1, 2, 6, 2, 6, 2, 2, 2, 2, 6)],
        ],
        compiler_params=pltpu.CompilerParams(
            collective_id=0, has_side_effects=True, vmem_limit_bytes=48 << 20
        ),
        cost_estimate=pl.CostEstimate(
            flops=6 * TOK * ROWS * D, bytes_accessed=4 * TOK * D, transcendentals=TOK * ROWS
        ),
    )(*[pltpu.with_memory_space_constraint(a, pltpu.HBM) for a in arguments])
    return loss.reshape(TOK), grad


def solution(mesh):
    placed = (P("dp", "tensor"), P(("dp", "tensor"), None), P("dp"), P("dp"))
    return jax.shard_map(
        body, mesh=mesh, in_specs=placed, out_specs=(P("dp"), P("dp", "tensor")), check_vma=False
    )
```

```python
import functools

import jax
import jax.numpy as jnp
from jax import lax
from jax.experimental import pallas as pl
from jax.experimental.pallas import tpu as pltpu
from jax.sharding import PartitionSpec as P

MESH = pl.DeviceIdType.MESH
BF16 = jnp.bfloat16
F32 = jnp.float32
NX, NY, NZ, NK = 4, 8, 8, 4
D = 5376
QUARTER = D // NK
MAIN = QUARTER // 128 * 128
REST = QUARTER - MAIN
PART_A = 768
WIDTHS = (PART_A, QUARTER - PART_A)
KEPT = 5
SPLIT = 18 * 128
TOK = 128
SET = TOK // NK
SUB = SET // 2
PIECE = 16
BLOCK = 8 * PIECE
ROWS = NY * NZ * PIECE


STEPS = (
    (
        ("first", 1, 3, False), ("send", 1), ("send", 3), ("send", 2), ("outer", 0), ("outer", 1),
        ("first", 3, 8, False), ("outer", 2), ("outer", 3), ("outer", 4), ("pass", 1), ("pass", 3),
        ("pass", 2), ("outer", 5), ("outer", 6), ("outer", 7), ("second", 1, 0, 8),
        ("second", 2, 0, 5), ("features",), ("own", 0), ("sibling", 0), ("second", 2, 5, 8),
        ("own", 1), ("second", 3, 0, 4), ("sibling", 1), ("own", 2), ("second", 3, 4, 8),
        ("sibling", 2), ("own", 3), ("sibling", 3), ("opposite",), ("own", 4), ("sibling", 4),
    ),
    (
        ("outer", 0), ("first", 1, 3, True), ("send", 1), ("send", 3), ("send", 2),
        ("second", 1, 0, 1), ("first", 3, 5, True), ("second", 2, 0, 1), ("pass", 1), ("pass", 3),
        ("pass", 2), ("second", 1, 1, 5), ("first", 5, 8, True), ("second", 2, 1, 5),
        ("second", 1, 5, 8), ("features",), ("own", 0), ("sibling", 0), ("own", 1),
        ("second", 2, 5, 8), ("second", 3, 0, 4), ("sibling", 1), ("own", 2), ("second", 3, 4, 8),
        ("sibling", 2), ("own", 3), ("sibling", 3), ("opposite",), ("own", 4), ("sibling", 4),
    ),
)


def device(x, y, z, c):
    return (((z % 2) * NX + x) * NY + y) * 2 + c, z // 2


def at_row(row):
    return pl.ds(pl.multiple_of(row * PIECE, PIECE), PIECE)


def ring_offset(m):
    return ((m + 1) // 2) * (1 - 2 * (m % 2))


def rearranged(quarters):
    return jnp.concatenate(
        [q[:, :MAIN] for q in quarters] + [q[:, MAIN:] for q in quarters], axis=1
    )


def kernel(
    hid_hbm, emb_hbm, tgt_hbm, pri_hbm, loss, out,
    hid, emb, tgt, pri, g, ebuf, hidn, hb, ht, lt, gl, raw, coef, meta, stat, lbuf,
    part_a, part_b, r1_a, r1_b, s2_a, s2_b, rd_a, rd_b, r3_a, r3_b, zs_a, zs_b, zr_a, zr_b,
    in_s, e_s, g_r, s_r, g_s, s_s, ha_s, ha_r, hx_s, hx_r,
    m_s, m_r, t_s, t_r, l_s, l_r, o_s, o_r, d_s, d_r, q_s, w_s, w_r, z_s, z_r,
):
    dp = lax.axis_index("dp")
    k = lax.axis_index("tensor")
    c = dp % 2
    y = dp // 2 % NY
    x = dp // (2 * NY) % NX
    zl = dp // (2 * NY * NX)
    z = 2 * k + zl

    def x_dev(d):
        return device((x + d) % NX, y, z, c)

    def k_dev(kk):
        return device(x, y, 2 * kk + zl, c)

    sibling = device(x, y, z, 1 - c)

    arguments = [
        pltpu.make_async_copy(src, dst, in_s.at[n])
        for n, (src, dst) in enumerate(((hid_hbm, hid), (emb_hbm, emb), (tgt_hbm, tgt), (pri_hbm, pri)))
    ]
    for argument in arguments:
        argument.start()

    partners = [sibling]
    partners += [device(x, (y + d) % NY, z, c) for d in (1, 2, 6, 7)]
    partners += [device(x, y, (z + d) % NZ, c) for d in (1, 2, 4, 6, 7)]
    partners += [x_dev(d) for d in (1, 2, 3)]
    barrier = pltpu.get_barrier_semaphore()
    for partner in partners:
        pl.semaphore_signal(barrier, inc=1, device_id=partner, device_id_type=MESH)

    for argument in arguments:
        argument.wait()
    for lo in range(0, QUARTER, 128):
        hi = min(lo + 128, QUARTER)
        hidn[:, lo:hi] = hid[lo:hi, :].astype(F32).T.astype(BF16)
    t = tgt[...]
    b = t // 8
    t_dp, t_k = b // 4, b % 4
    t_z = 2 * t_k + t_dp // (2 * NY * NX)
    place = (t_dp // (2 * NY) % NX) * ROWS + (t_z * NY + t_dp // 2 % NY) * PIECE + t_dp % 2 * 8 + t % 8
    meta[x] = jnp.concatenate([place.astype(F32), pri[...], jnp.zeros((6, TOK), F32)], axis=0)
    pl.semaphore_wait(barrier, len(partners))

    def received(ref, recv):
        copy(ref, ref, e_s.at[0], recv, sibling).wait_recv()

    def sent(ref, send):
        copy(ref, ref, send, e_s.at[1], sibling).wait_send()

    def copy(src, dst, send, recv, where):
        return pltpu.make_async_remote_copy(
            src_ref=src, dst_ref=dst, send_sem=send, recv_sem=recv,
            device_id=where, device_id_type=MESH,
        )

    e_copy = copy(emb, ebuf, e_s.at[0], e_s.at[1], sibling)
    e_copy.start()

    def set_rows(kk):
        return pl.ds(pl.multiple_of(kk * SET, SET), SET)

    def hidden_set(d):
        kk = (k + d) % NK
        return copy(hidn.at[set_rows(kk)], hb.at[x, k], ha_s.at[0], ha_r.at[d - 1], k_dev(kk))

    def hidden_x(j, d):
        ref = hb.at[x, j]
        return copy(ref, ref, hx_s.at[0], hx_r.at[0], x_dev(d))

    def hidden_on(d):
        received(hb.at[x, (k + NK - d) % NK], ha_r.at[d - 1])
        for e in (1, 3, 2):
            hidden_x((k + NK - d) % NK, e).start()

    def to_x(buf, send, recv, d):
        return copy(buf.at[x], buf.at[x], send.at[0], recv.at[0], x_dev(d))

    hb[x, k] = hidn[set_rows(k), :]
    e_copy.wait()
    mine, other = emb[...], ebuf[...]
    rows = jnp.concatenate(
        [jnp.where(c == 0, mine, other), jnp.where(c == 0, other, mine)], axis=0
    )
    g[at_row(z * NY + y), :] = rearranged(
        [rows[:, j * QUARTER:(j + 1) * QUARTER] for j in range(NK)]
    )

    def bring_in(h):
        outer, inner = (z, y) if h == 0 else (y, z)
        spans = (slice(0, SPLIT), slice(SPLIT, D))

        def number(o, i):
            return o * 8 + i if h == 0 else i * 8 + o

        def ring_dev(o, i):
            return device(x, i, o, c) if h == 0 else device(x, o, i, c)

        outer_next = ring_dev((outer + 1) % 8, inner)
        outer_last = ring_dev((outer + 7) % 8, inner)

        def piece(n, share):
            return g.at[at_row(n), spans[share]]

        def to_ring(o, i, where, recv):
            ref = piece(number(o, i), h)
            copy(ref, ref, g_s.at[0], g_r.at[recv], where).start()

        def to_inner(i, d, recv):
            to_ring(outer, i, ring_dev(outer, (inner + d + 8) % 8), recv)

        def to_sibling(o, i):
            ref = piece(number(o, i), h)
            copy(ref, ref, s_s.at[0], s_r.at[o], sibling).start()

        def to_outer(m):
            i = (inner + ring_offset(m) + 8) % 8
            to_ring(outer, i, outer_next, 8 + m)
            to_ring(outer, i, outer_last, 8 + m)

        for m, d in ((1, 1), (2, -1), (3, 2), (4, -2)):
            to_inner(inner, d, m)
        for e in (1, 3, 2):
            hidden_x(k, e).start()
        for d in (1, 2, 3):
            to_x(meta, m_s, m_r, d).start()

        def first(start, end, outward):
            for m in range(start, end):
                i = (inner + ring_offset(m) + 8) % 8
                received(piece(number(outer, i), h), g_r.at[m])
                for to, d in {3: ((5, 1), (7, 2)), 4: ((6, -1),)}.get(m, ()):
                    to_inner(i, d, to)
                if outward:
                    to_outer(m)
                to_sibling(outer, i)

        def second(ring, start, end):
            up, down = (outer + 8 - ring) % 8, (outer + ring) % 8

            def step(m, carry):
                i = (inner + ring_offset(m) + 8) % 8
                received(g.at[0:2 * PIECE, spans[h]], g_r.at[ring * 8 + m])
                to = (ring + 1) * 8 + m
                if ring == 3:
                    pl.when(m % 2 == 1)(lambda: to_ring(up, i, outer_next, to))
                    pl.when(m % 2 == 0)(lambda: to_ring(down, i, outer_last, to))
                else:
                    to_ring(up, i, outer_next, to)
                    to_ring(down, i, outer_last, to)
                to_sibling(up, i)
                to_sibling(down, i)
                return carry

            lax.fori_loop(start, end, step, 0)

        def logits(share, offsets):
            o0 = outer if share == h else inner
            by_z = share == 0
            starts = []
            for r in offsets:
                o = (o0 + r) % 8
                if by_z:
                    starts.append((pl.multiple_of(o * BLOCK, BLOCK), BLOCK))
                else:
                    starts += [(pl.multiple_of((i * 8 + o) * PIECE, PIECE), PIECE) for i in range(8)]
            left = jnp.concatenate([g[pl.ds(a, n), spans[share]] for a, n in starts], axis=0)
            value = lax.dot_general(
                left, ht[:, spans[share]], (((1,), (1,)), ((), ())), preferred_element_type=F32
            )
            at = 0
            for a, n in starts:
                lt[share, pl.ds(a, n), :] = value[at:at + n]
                at += n

        def await_sibling(r):
            rows = BLOCK - PIECE if isinstance(r, int) and r == 0 else BLOCK
            received(g.at[0:rows, spans[1 - h]], s_r.at[(inner + r) % 8])

        def features():
            received(hb.at[0:NX - 1], hx_r.at[0])
            for xx in range(NX):
                ht[xx * SET:(xx + 1) * SET, :] = rearranged([hb[xx, j] for j in range(NK)])

        def own_logits(r):
            logits(h, (r,) if r % 4 == 0 else (r, 8 - r))

        def sibling_logits(r):
            for b in (r,) if r % 4 == 0 else (r, 8 - r):
                await_sibling(b)
            logits(1 - h, (r,) if r % 4 == 0 else (r, 8 - r))

        def opposite():
            across = (outer + 4) % 8
            for m in range(8):
                i = (inner + ring_offset(m) + 8) % 8
                received(piece(number(across, i), h), g_r.at[32 + m])
                to_sibling(across, i)

        acts = {
            "first": first, "outer": to_outer, "second": second, "opposite": opposite,
            "send": lambda d: hidden_set(d).start(), "pass": hidden_on, "features": features,
            "own": own_logits, "sibling": sibling_logits,
        }
        for act, *numbers in STEPS[h]:
            acts[act](*numbers)

        sent(g.at[0:ROWS - PIECE, spans[h]], g_s.at[0])
        sent(g.at[0:ROWS - PIECE, spans[h]], s_s.at[0])

    for core in (0, 1):
        pl.when(c == core)(functools.partial(bring_in, core))

    lane_set = lax.broadcasted_iota(jnp.int32, (8, TOK), 1) // SET
    received(meta.at[0:NX - 1], m_r.at[0])
    info = jnp.zeros((8, TOK), F32)
    for xx in range(NX):
        turned = pltpu.roll(meta[xx], (xx + NX - k) % NX * SET, axis=1)
        info = jnp.where(lane_set == xx, turned, info)
    column = info[0:1] - (x * ROWS).astype(F32)
    owned = (column >= 0.0) & (column < float(ROWS))
    prior = info[1:2]

    peaks = jnp.full((8, TOK), -jnp.inf, F32)
    for n in range(8):
        span = slice(n * BLOCK, (n + 1) * BLOCK)
        value = lt[0, span, :] + lt[1, span, :]
        lt[0, span, :] = value
        peaks = jnp.maximum(peaks, jnp.max(value.reshape(BLOCK // 8, 8, TOK), axis=0))
    peak = jnp.max(peaks, axis=0, keepdims=True)
    total = jnp.zeros((8, TOK), F32)
    target = jnp.zeros((8, TOK), F32)
    row_id = lax.broadcasted_iota(jnp.int32, (BLOCK, TOK), 0).astype(F32)
    for n in range(8):
        span = slice(n * BLOCK, (n + 1) * BLOCK)
        value = lt[0, span, :]
        hit = row_id == column - float(n * BLOCK)
        power = jnp.exp(value - peak)
        lt[1, span, :] = jnp.where(hit, 0.0, power)
        total += jnp.sum(power.reshape(BLOCK // 8, 8, TOK), axis=0)
        target += jnp.sum(jnp.where(hit, value, 0.0).reshape(BLOCK // 8, 8, TOK), axis=0)
    my_target = jnp.sum(target, axis=0, keepdims=True)
    stat[x] = jnp.concatenate(
        [peak, jnp.sum(total, axis=0, keepdims=True), my_target, jnp.zeros((5, TOK), F32)], axis=0
    )
    for d in (1, 2, 3):
        to_x(stat, t_s, t_r, d).start()

    column_t = jnp.broadcast_to(column, (8, TOK)).T[:, 0:1]
    lane_id = lax.broadcasted_iota(jnp.int32, (TOK, BLOCK), 1).astype(F32)
    for n in range(8):
        span = slice(n * BLOCK, (n + 1) * BLOCK)
        gl[0:TOK, span] = lt[1, span, :].T.astype(BF16)
        gl[TOK:, span] = jnp.where(lane_id == column_t - float(n * BLOCK), 1.0, 0.0).astype(BF16)

    units = ((2, 1), (2, 0), (1, 0), (3, 0), (1, 1), (3, 1), (0, 0), (0, 1))
    turns = (2, 1, 3, 0)
    parts, r1s, s2s, rds = (part_a, part_b), (r1_a, r1_b), (s2_a, s2_b), (rd_a, rd_b)
    r3s, zss, zrs = (r3_a, r3_b), (zs_a, zs_b), (zr_a, zr_b)

    def place_of(u):
        turn, p = units[u]
        return turns.index(turn), p

    def products(u, use):
        turn, p = units[u]
        j = (k + turn) % NK
        for lo, hi in ((0, 512), (512, PART_A)) if p == 0 else ((PART_A, MAIN),):
            at = pl.ds(pl.multiple_of(j * MAIN + lo, 128), hi - lo)
            use(lo - p * PART_A, jnp.dot(gl[...], g[:, at], preferred_element_type=F32))
        if p == 1:
            at = pl.ds(pl.multiple_of(NK * MAIN + j // 2 * 128, 128), 128)
            value = jnp.dot(gl[...], g[:, at], preferred_element_type=F32)
            use(MAIN - PART_A, pltpu.roll(value, j % 2 * REST, axis=1)[:, :REST])

    def weigh(u):
        q, p = place_of(u)

        def use(lo, value):
            for at in range(0, value.shape[1], 128):
                w = min(128, value.shape[1] - at)
                mixed = (
                    value[:TOK, at:at + w] * coef[0, :, :w] + value[TOK:, at:at + w] * coef[1, :, :w]
                )
                parts[p][q, :, lo + at:lo + at + w] = mixed.astype(BF16)

        return use

    def keep(u):
        def use(lo, value):
            raw[u, :, lo:lo + value.shape[1]] = value

        return use

    for u in range(KEPT):
        products(u, keep(u))

    received(stat.at[0:NX - 1], t_r.at[0])
    top = prior
    for xx in range(NX):
        top = jnp.maximum(top, stat[xx, 0:1, :])
    whole = jnp.exp(prior - top)
    logit = jnp.zeros((1, TOK), F32)
    for xx in range(NX):
        whole += stat[xx, 1:2, :] * jnp.exp(stat[xx, 0:1, :] - top)
        logit += stat[xx, 2:3, :]
    lse = top + jnp.log(whole)
    weights = jnp.concatenate(
        [jnp.exp(peak - lse), jnp.where(owned, jnp.exp(my_target - lse) - 1.0, 0.0),
         jnp.zeros((6, TOK), F32)], axis=0,
    ).T
    coef[0] = jnp.broadcast_to(weights[:, 0:1], (TOK, 128))
    coef[1] = jnp.broadcast_to(weights[:, 1:2], (TOK, 128))

    def x_rows(d):
        return pl.ds(pl.multiple_of((x + d) % NX * SET, SET), SET)

    def x_half(d, way):
        return pl.ds(pl.multiple_of((x + d) % NX * SET + way * SUB, SUB), SUB)

    ways = ((0, 1, 3), (1, 3, 1))

    def opposite_copy(u, way, d):
        q, p = place_of(u)
        return copy(parts[p].at[q, x_half(2, way)], r1s[p].at[q, way], o_s.at[p], o_r.at[u], x_dev(d))

    def direct_copy(u, way, d):
        q, p = place_of(u)
        return copy(parts[p].at[q, x_half(d, way)], rds[p].at[q, way], d_s.at[p], d_r.at[u], x_dev(d))

    def sum_copy(u, way, d):
        q, p = place_of(u)
        return copy(s2s[p].at[q, way], rds[p].at[q, 2 + way], q_s.at[p], d_r.at[u], x_dev(d))

    def straight_copy(p, d):
        return copy(parts[p].at[3, x_rows(d)], r3s[p].at[d - 1], w_s.at[p], w_r.at[p], x_dev(d))

    def z_copy(u):
        q, p = place_of(u)
        return copy(zss[p].at[q], zrs[p].at[q], z_s.at[p], z_r.at[u], k_dev((k + units[u][0]) % NK))

    def send_first(u):
        q, p = place_of(u)
        if q == 3:
            for d in (2, 1, 3):
                straight_copy(p, d).start()
            return
        for way, near, _ in ways:
            opposite_copy(u, way, near).start()
        for way, _, far in ways:
            direct_copy(u, way, far).start()

    def multiply(u):
        _, p = place_of(u)
        for lo in range(0, WIDTHS[p], 128):
            weigh(u)(lo, raw[u, :, lo:min(lo + 128, WIDTHS[p])])
        send_first(u)

    def add_first(u):
        q, p = place_of(u)
        received(r1s[p].at[q], o_r.at[u])
        for way, near, _ in ways:
            s2s[p][q, way] = (
                parts[p][q, x_half(near, way), :].astype(F32) + r1s[p][q, way].astype(F32)
            ).astype(BF16)
            sum_copy(u, way, near).start()

    def add_last(u):
        q, p = place_of(u)
        received(rds[p].at[q], d_r.at[u])
        for way in (0, 1):
            zss[p][q, way * SUB:(way + 1) * SUB, :] = (
                parts[p][q, x_half(0, way), :].astype(F32)
                + rds[p][q, way].astype(F32) + rds[p][q, 2 + way].astype(F32)
            ).astype(BF16)
        z_copy(u).start()

    def own(p):
        received(r3s[p], w_r.at[p])
        value = parts[p][3, x_rows(0), :].astype(F32)
        for d in (1, 2, 3):
            value += r3s[p][d - 1].astype(F32)
        out[set_rows(k), p * PART_A:p * PART_A + WIDTHS[p]] = value.astype(BF16)

    def finish(u):
        q, p = place_of(u)
        received(zrs[p].at[q], z_r.at[u])
        rows = set_rows((k + NK - units[u][0]) % NK)
        out[rows, p * PART_A:p * PART_A + WIDTHS[p]] = zrs[p][q]

    multiply(0)
    lbuf[k] = jnp.broadcast_to(lse - logit, (8, TOK))

    def loss_to(d):
        return copy(lbuf.at[k], lbuf.at[k], l_s.at[0], l_r.at[0], k_dev((k + d) % NK))

    for d in (1, 2, 3):
        loss_to(d).start()
    multiply(1)
    multiply(2)
    for u in range(KEPT, 8):
        products(u, keep(u))
    add_first(0)
    multiply(3)
    add_first(1)
    multiply(4)
    add_first(2)
    multiply(5)
    add_first(3)
    add_last(0)
    add_first(4)
    add_last(1)
    add_first(5)
    add_last(2)
    add_last(3)
    @pl.when(c == 0)
    def _():
        multiply(6)

    add_last(4)

    @pl.when(c == 0)
    def _():
        multiply(7)

    add_last(5)

    @pl.when(c == 1)
    def _():
        multiply(6)
        multiply(7)

    received(lbuf.at[0:NK - 1], l_r.at[0])
    result = jnp.zeros((8, TOK), F32)
    for kk in range(NK):
        turned = pltpu.roll(lbuf[kk], (kk + NX - x) % NX * SET, axis=1)
        result = jnp.where(lane_set == kk, turned, result)
    loss[...] = result[0:1]

    finish(0)
    finish(1)
    own(0)
    own(1)
    for u in (2, 4, 3, 5):
        finish(u)

    sent(hidn.at[0:TOK - SET], ha_s.at[0])
    sent(hb.at[0:NX - 1], hx_s.at[0])
    for buf, send in ((meta, m_s), (stat, t_s), (lbuf, l_s)):
        sent(buf.at[0:3], send.at[0])
    for p in (0, 1):
        sent(r1s[p], o_s.at[p])
        sent(r1s[p], d_s.at[p])
        sent(r1s[p], q_s.at[p])
        sent(r3s[p], w_s.at[p])
        sent(zss[p], z_s.at[p])


def body(hidden_states, embedding, targets, prior_lse):
    dma = pltpu.SemaphoreType.DMA
    hbm = pl.BlockSpec(memory_space=pltpu.HBM)
    vmem = pl.BlockSpec(memory_space=pltpu.VMEM)
    arguments = (hidden_states.T, embedding, targets.reshape(1, TOK), prior_lse.reshape(1, TOK))
    pair = [(WIDTHS[0],), (WIDTHS[1],)]
    loss, grad = pl.pallas_call(
        kernel,
        out_shape=(
            jax.ShapeDtypeStruct((1, TOK), F32),
            jax.ShapeDtypeStruct((TOK, QUARTER), BF16),
        ),
        in_specs=[hbm] * 4,
        out_specs=(vmem, vmem),
        scratch_shapes=[
            pltpu.VMEM((QUARTER, TOK), BF16),
            pltpu.VMEM((8, D), BF16),
            pltpu.VMEM((1, TOK), jnp.int32),
            pltpu.VMEM((1, TOK), F32),
            pltpu.VMEM((ROWS, D), BF16),
            pltpu.VMEM((8, D), BF16),
            pltpu.VMEM((TOK, QUARTER), BF16),
            pltpu.VMEM((NX, NK, SET, QUARTER), BF16),
            pltpu.VMEM((TOK, D), BF16),
            pltpu.VMEM((2, ROWS, TOK), F32),
            pltpu.VMEM((2 * TOK, ROWS), BF16),
            pltpu.VMEM((8, 2 * TOK, WIDTHS[0]), F32),
            pltpu.VMEM((2, TOK, 128), F32),
            pltpu.VMEM((NX, 8, TOK), F32),
            pltpu.VMEM((NX, 8, TOK), F32),
            pltpu.VMEM((NK, 8, TOK), F32),
            *[pltpu.VMEM((NK, TOK) + w, BF16) for w in pair],
            *[pltpu.VMEM((NK - 1, 2, SUB) + w, BF16) for w in pair * 2],
            *[pltpu.VMEM((NK - 1, 4, SUB) + w, BF16) for w in pair],
            *[pltpu.VMEM((NX - 1, SET) + w, BF16) for w in pair],
            *[pltpu.VMEM((NK - 1, SET) + w, BF16) for w in pair * 2],
            *[dma((n,)) for n in (4, 2, 40, 8, 1, 1, 1, 3, 1, 1)],
            *[dma((n,)) for n in (1, 1, 1, 1, 1, 1, 2, 6, 2, 6, 2, 2, 2, 2, 6)],
        ],
        compiler_params=pltpu.CompilerParams(
            collective_id=0, has_side_effects=True, vmem_limit_bytes=48 << 20
        ),
        cost_estimate=pl.CostEstimate(
            flops=6 * TOK * ROWS * D, bytes_accessed=4 * TOK * D, transcendentals=TOK * ROWS
        ),
    )(*[pltpu.with_memory_space_constraint(a, pltpu.HBM) for a in arguments])
    return loss.reshape(TOK), grad


def solution(mesh):
    placed = (P("dp", "tensor"), P(("dp", "tensor"), None), P("dp"), P("dp"))
    return jax.shard_map(
        body, mesh=mesh, in_specs=placed, out_specs=(P("dp"), P("dp", "tensor")), check_vma=False
    )
```
